128 devices in a mesh: gx: 16 (over z, y_hi, core), gy: 8 (over x, y_lo).
Axes of the slice: x: 4, y: 4 (y_hi: 2, y_lo: 2; y = y_hi * 2 + y_lo), z: 4, core: 2. Of those that a mesh axis runs over, the one named last changes fastest.
Arguments:
- residents: float32 [16, 64, 32768], P(None, 'gx', 'gy'), as said below
- cell_count: int32 [64, 8192], P('gx', 'gy'), may hold values from 0 to 4, as said below
- outbox: float32 [16, 64, 2048], P(None, 'gx', 'gy'), as said below
- corner_box: float32 [16, 64, 512], P(None, 'gx', 'gy'), as said below
- face_cell: int32 [64, 2048], P('gx', 'gy'), may hold values from 0 to 4095, as said below
- corner_cell: int32 [64, 512], P('gx', 'gy'), may hold values from 0 to 4095, as said below
- mig_count: int32 [128, 8], P('gx', 'gy'), may hold values from 0 to 256, as said below
Outputs:
- resident_next: float32 [16, 64, 32768], P(None, 'gx', 'gy')
- migrant_next: float32 [16, 64, 2048], P(None, 'gx', 'gy')
- corner_next: float32 [16, 64, 512], P(None, 'gx', 'gy')
The draws below stay inside these ranges and needn't reach their ends.
Inputs may be any that keep to these rules, and one draw needn't show every extreme that they name: `residents`: rows 0 to 2 lie in [-0.5, 0.5) and row 15 is positive. `outbox`: rows 0 to 2 lie in [-0.5, 0.5) and row 15 is positive. `corner_box`: rows 0 to 2 lie in [-0.5, 0.5) and row 15 is positive. `cell_count`: cells with z = 0 or z = 63 hold no particle; some cell holds 4. `face_cell`: A migrant's cell lies on the face of the receiving tile through which it enters (x = 0 when sx = 1, x = 3 when sx = -1, likewise y), with 1 <= z <= 62. `corner_cell`: A diagonal migrant's cell lies on the corner column of the receiving tile through which it enters, with 1 <= z <= 62. `mig_count`: face directions count at most 256 and diagonal ones at most 64; some tile sends 256 toward some face direction and some tile sends 64 toward some diagonal direction.
All inputs are finite; a program needn't handle non-finite values.
Results may differ from the reference program's by a relative error of at most 0.0003.
Values sent between devices are 32-bit elements; how exact they have to be, the bound alone decides.
No kernel may reach another device: no remote copies, remote signals or barrier semaphores. Data moves between devices by JAX's collectives and lax.ppermute only.
A program may use at most 128 MiB of HBM per device.

```python
import math
import jax
import jax.numpy as jnp
from jax import lax

CX = 4
CY = 16
NZ = 64
BIN = 4
MIG = 256
CORNER = 64
TILES_X = 16
TILES_Y = 8
NX = 64
NY = 128
ROUTE_ROWS = 128
FACE_ROWS = 64
FACE_SLOTS = 2048
CORNER_SLOTS = 512


FACE_DIRS = ((1, 0), (-1, 0), (0, 1), (0, -1))


CORNER_DIRS = ((1, 1), (1, -1), (-1, 1), (-1, -1))


def draw_particles(key, row_count, column_count):
    subkeys = jax.random.split(key, 4)
    dims = (row_count, column_count)
    offset = jax.random.uniform(subkeys[0], (3,) + dims, jnp.float32, -0.5, 0.5)
    velocity = jnp.clip(jax.random.normal(subkeys[1], (3,) + dims, jnp.float32), -6.0, 6.0)
    affine = 0.5 * jnp.clip(jax.random.normal(subkeys[2], (9,) + dims, jnp.float32), -6.0, 6.0)
    masses = jnp.exp(jax.random.uniform(subkeys[3], (1,) + dims, jnp.float32, math.log(0.2), math.log(2.0)))
    return jnp.concatenate([offset, velocity, affine, masses], axis=0)


def draw_residents(key, part):
    return draw_particles(key, NX, NY * BIN * NZ)


def draw_outbox(key, part):
    return draw_particles(key, FACE_ROWS, FACE_SLOTS)


def draw_corner_box(key, part):
    return draw_particles(key, FACE_ROWS, CORNER_SLOTS)


def draw_cell_count(key, part):
    subkeys = jax.random.split(key, 5)
    full_shape = (TILES_X, CX, TILES_Y, CY, NZ)
    tile_caps = jax.random.randint(subkeys[0], (TILES_X, 1, TILES_Y, 1, 1), 1, BIN + 1)
    raw_counts = jax.random.randint(subkeys[1], full_shape, 0, BIN + 1)
    layer_index = lax.broadcasted_iota(jnp.int32, full_shape, 4)
    inside = (layer_index > 0) & (layer_index < NZ - 1)
    counts = jnp.where(inside, jnp.minimum(raw_counts, tile_caps), 0).reshape(NX, NY * NZ)
    row_pick = jax.random.randint(subkeys[2], (), 0, NX)
    column_pick = jax.random.randint(subkeys[3], (), 0, NY)
    depth_pick = jax.random.randint(subkeys[4], (), 1, NZ - 1)
    return counts.at[row_pick, column_pick * NZ + depth_pick].set(BIN)


def draw_cells(key, directions, capacity):
    subkeys = jax.random.split(key, 3)
    slot_shape = (TILES_X, 4, TILES_Y, capacity)
    step_x = jnp.array([pair[0] for pair in directions], jnp.int32).reshape(1, 4, 1, 1)
    step_y = jnp.array([pair[1] for pair in directions], jnp.int32).reshape(1, 4, 1, 1)
    across_x = jax.random.randint(subkeys[0], slot_shape, 0, CX)
    across_y = jax.random.randint(subkeys[1], slot_shape, 0, CY)
    depth_cell = jax.random.randint(subkeys[2], slot_shape, 1, NZ - 1)
    cell_x = jnp.where(step_x == 1, 0, jnp.where(step_x == -1, CX - 1, across_x))
    cell_y = jnp.where(step_y == 1, 0, jnp.where(step_y == -1, CY - 1, across_y))
    places = cell_x * (CY * NZ) + cell_y * NZ + depth_cell
    return places.reshape(FACE_ROWS, TILES_Y * capacity)


def draw_face_cell(key, part):
    return draw_cells(key, FACE_DIRS, MIG)


def draw_corner_cell(key, part):
    return draw_cells(key, CORNER_DIRS, CORNER)


def draw_mig_count(key, part):
    subkeys = jax.random.split(key, 7)
    count_shape = (TILES_X, 8, TILES_Y)
    direction = lax.broadcasted_iota(jnp.int32, count_shape, 1)
    top = jnp.where(direction < 4, MIG, CORNER)
    low = top // 3
    raw = jax.random.randint(subkeys[0], count_shape, 0, 1 << 20)
    counts = low + raw % (top - low + 1)
    face_x = jax.random.randint(subkeys[1], (), 0, TILES_X)
    face_d = jax.random.randint(subkeys[2], (), 0, 4)
    face_y = jax.random.randint(subkeys[3], (), 0, TILES_Y)
    counts = counts.at[face_x, face_d, face_y].set(MIG)
    corner_x = jax.random.randint(subkeys[4], (), 0, TILES_X)
    corner_d = jax.random.randint(subkeys[5], (), 4, 8)
    corner_y = jax.random.randint(subkeys[6], (), 0, TILES_Y)
    counts = counts.at[corner_x, corner_d, corner_y].set(CORNER)
    return counts.reshape(ROUTE_ROWS, TILES_Y)


def setup_inputs(seed: int = 0) -> dict:
    seeds = jax.random.split(jax.random.key(seed), 8)
    residents = draw_residents(jax.random.fold_in(seeds[7], 71), 0)
    cell_count = draw_cell_count(jax.random.fold_in(seeds[7], 71), 0)
    outbox = draw_outbox(jax.random.fold_in(seeds[7], 71), 0)
    corner_box = draw_corner_box(jax.random.fold_in(seeds[7], 71), 0)
    face_cell = draw_face_cell(jax.random.fold_in(seeds[7], 71), 0)
    corner_cell = draw_corner_cell(jax.random.fold_in(seeds[7], 71), 0)
    mig_count = draw_mig_count(jax.random.fold_in(seeds[7], 71), 0)
    return dict(residents=residents, cell_count=cell_count, outbox=outbox, corner_box=corner_box, face_cell=face_cell, corner_cell=corner_cell, mig_count=mig_count)


FACE_DIRS = ((1, 0), (-1, 0), (0, 1), (0, -1))
CORNER_DIRS = ((1, 1), (1, -1), (-1, 1), (-1, -1))
STENCIL = tuple((step_x, step_y, step_z) for step_x in (-1, 0, 1) for step_y in (-1, 0, 1) for step_z in (-1, 0, 1))
time_step = 0.1
gravity = 1.0
mass_floor = 0.5


def spline(offset):
    return (0.5 * (0.5 - offset) ** 2, 0.75 - offset * offset, 0.5 * (0.5 + offset) ** 2)


def particle_terms(particle, living):
    masses = particle[15] * living
    carried = []
    for channel in range(3):
        skewed = particle[6 + 3 * channel] * particle[0] + particle[7 + 3 * channel] * particle[1] + particle[8 + 3 * channel] * particle[2]
        carried.append(masses * (particle[3 + channel] - skewed))
    splines = (spline(particle[0]), spline(particle[1]), spline(particle[2]))
    return masses, carried, splines


def offset_terms(particle, masses, carried, splines, offsets):
    weight = splines[0][offsets[0] + 1] * splines[1][offsets[1] + 1] * splines[2][offsets[2] + 1]
    row_terms = [weight * masses]
    for channel in range(3):
        turned = offsets[0] * particle[6 + 3 * channel] + offsets[1] * particle[7 + 3 * channel] + offsets[2] * particle[8 + 3 * channel]
        row_terms.append(weight * (carried[channel] + masses * turned))
    return weight, jnp.stack(row_terms, axis=0)


def velocity_terms(particle, weight, node_values, offsets, new_velocity, new_affine):
    for channel in range(3):
        weighted = weight * node_values[channel]
        new_velocity[channel] = new_velocity[channel] + weighted
        for column in range(3):
            new_affine[3 * channel + column] = new_affine[3 * channel + column] + 4.0 * weighted * (offsets[column] - particle[column])


def finish(particle, living, new_velocity, new_affine):
    shifted = [particle[coordinate] + time_step * new_velocity[coordinate] for coordinate in range(3)]
    return jnp.stack(shifted + new_velocity + new_affine + [particle[15]], axis=0) * living


def arrive(box, cells, tallies, directions, capacity):
    movers = box.reshape(16, TILES_X, 4, TILES_Y, capacity)
    targets = cells.reshape(TILES_X, 4, TILES_Y, capacity)
    moved_states = []
    moved_places = []
    moved_tallies = []
    for position in range(4):
        shift_pair = directions[position]
        moved_states.append(jnp.roll(movers[:, :, position], shift_pair, axis=(1, 2)))
        moved_places.append(jnp.roll(targets[:, position], shift_pair, axis=(0, 1)))
        moved_tallies.append(jnp.roll(tallies[:, position], shift_pair, axis=(0, 1)))
    states = jnp.stack(moved_states, axis=2).reshape(16, -1)
    places = jnp.stack(moved_places, axis=1)
    tallies_in = jnp.stack(moved_tallies, axis=1)
    slot_shape = (TILES_X, 4, TILES_Y, capacity)
    slot_mig = lax.broadcasted_iota(jnp.int32, slot_shape, 3)
    living = (slot_mig < tallies_in[:, :, :, None]).astype(jnp.float32).reshape(-1)
    tile_x = lax.broadcasted_iota(jnp.int32, slot_shape, 0)
    tile_y = lax.broadcasted_iota(jnp.int32, slot_shape, 2)
    global_x = (tile_x * CX + places // (CY * NZ)).reshape(-1)
    global_y = (tile_y * CY + (places // NZ) % CY).reshape(-1)
    depth_cell = (places % NZ).reshape(-1)
    return states, living, global_x, global_y, depth_cell


def reference(residents, cell_count, outbox, corner_box, face_cell, corner_cell, mig_count):
    particle = residents.reshape(16, NX, NY, BIN, NZ)
    slot_rank = lax.broadcasted_iota(jnp.int32, (NX, NY, BIN, NZ), 2)
    living = (slot_rank < cell_count.reshape(NX, NY, 1, NZ)).astype(jnp.float32)
    tallies = mig_count.reshape(TILES_X, 8, TILES_Y)
    face_part = arrive(outbox, face_cell, tallies[:, :4], FACE_DIRS, MIG)
    corner_part = arrive(corner_box, corner_cell, tallies[:, 4:], CORNER_DIRS, CORNER)
    arrivals = jnp.concatenate([face_part[0], corner_part[0]], axis=1)
    mig_living = jnp.concatenate([face_part[1], corner_part[1]], axis=0)
    global_x = jnp.concatenate([face_part[2], corner_part[2]], axis=0)
    global_y = jnp.concatenate([face_part[3], corner_part[3]], axis=0)
    depth_cell = jnp.concatenate([face_part[4], corner_part[4]], axis=0)
    face_total = face_part[1].shape[0]

    masses, carried, splines = particle_terms(particle, living)
    mig_masses, mig_carried, mig_splines = particle_terms(arrivals, mig_living)
    grid_sums = jnp.zeros((4, NX, NY, NZ), jnp.float32)
    flat_grid = jnp.zeros((4, NX * NY * NZ), jnp.float32)
    for offsets in STENCIL:
        weight, deposit_terms = offset_terms(particle, masses, carried, splines, offsets)
        grid_sums = grid_sums + jnp.roll(jnp.sum(deposit_terms, axis=3), offsets, axis=(1, 2, 3))
        mig_weight, mig_terms = offset_terms(arrivals, mig_masses, mig_carried, mig_splines, offsets)
        node_index = ((global_x + offsets[0]) % NX) * (NY * NZ) + ((global_y + offsets[1]) % NY) * NZ + depth_cell + offsets[2]
        flat_grid = flat_grid.at[:, node_index].add(mig_terms)
    grid_sums = grid_sums + flat_grid.reshape(4, NX, NY, NZ)

    velocity = grid_sums[1:4] / jnp.maximum(grid_sums[0], mass_floor)[None]
    velocity = velocity - time_step * gravity * jnp.array([0.0, 0.0, 1.0], jnp.float32).reshape(3, 1, 1, 1)
    layer_index = lax.broadcasted_iota(jnp.int32, (1, NX, NY, NZ), 3)
    velocity = jnp.where((layer_index > 0) & (layer_index < NZ - 1), velocity, 0.0)
    flat_velocity = velocity.reshape(3, -1)

    new_velocity = [jnp.zeros_like(living) for channel in range(3)]
    new_affine = [jnp.zeros_like(living) for column in range(9)]
    mig_velocity = [jnp.zeros_like(mig_living) for channel in range(3)]
    mig_affine = [jnp.zeros_like(mig_living) for column in range(9)]
    for offsets in STENCIL:
        weight = splines[0][offsets[0] + 1] * splines[1][offsets[1] + 1] * splines[2][offsets[2] + 1]
        node_values = jnp.roll(velocity, (-offsets[0], -offsets[1], -offsets[2]), axis=(1, 2, 3))[:, :, :, None, :]
        velocity_terms(particle, weight, node_values, offsets, new_velocity, new_affine)
        mig_weight = mig_splines[0][offsets[0] + 1] * mig_splines[1][offsets[1] + 1] * mig_splines[2][offsets[2] + 1]
        node_index = ((global_x + offsets[0]) % NX) * (NY * NZ) + ((global_y + offsets[1]) % NY) * NZ + depth_cell + offsets[2]
        velocity_terms(arrivals, mig_weight, flat_velocity[:, node_index], offsets, mig_velocity, mig_affine)
    resident_next = finish(particle, living, new_velocity, new_affine).reshape(16, NX, NY * BIN * NZ)
    migrant_all = finish(arrivals, mig_living, mig_velocity, mig_affine)
    migrant_next = migrant_all[:, :face_total].reshape(16, FACE_ROWS, FACE_SLOTS)
    corner_next = migrant_all[:, face_total:].reshape(16, FACE_ROWS, CORNER_SLOTS)
    return resident_next, migrant_next, corner_next
```

```python
import jax
import jax.numpy as jnp
from jax import lax
from jax.experimental import pallas as pl
from jax.experimental.pallas import tpu as pltpu
from jax.sharding import PartitionSpec as P

CX = 4
CY = 16
NZ = 64
MIG = 256
CORNER = 64
PAIR = 2 * CORNER
WIDE = MIG + PAIR
YY = 20
YP = 24
Y_ROWS = 104
X_ROWS = 168
X_STATES = 112
time_step = 0.1
gravity = 1.0
mass_floor = 0.5
STEPS = (-1, 0, 1)
F32 = jnp.float32
BF16 = jnp.bfloat16


def spline(offset):
    low = 0.5 - offset
    high = 0.5 + offset
    return (0.5 * (low * low), 0.75 - offset * offset, 0.5 * (high * high))


def deposit_terms(state, living):
    mass = state[15] * living
    affine = [mass * state[6 + j] for j in range(9)]
    carried = []
    for i in range(3):
        skew = affine[3 * i] * state[0] + affine[3 * i + 1] * state[1] + affine[3 * i + 2] * state[2]
        carried.append(mass * state[3 + i] - skew)
    return mass, carried, affine


def placed(rows, width, cell, weights, wrap=None):
    row = lax.broadcasted_iota(jnp.int32, (rows, width), 0)
    step = row - cell
    if wrap is not None:
        step = jnp.where(step > wrap // 2, step - wrap, jnp.where(step < -wrap // 2, step + wrap, step))
    low, mid, high = weights
    zero = jnp.zeros((rows, width), F32)
    is_low, is_high = step == -1, step == 1
    moment = jnp.where(is_low, -low, jnp.where(is_high, high, zero))
    plain = jnp.where(is_low, low, jnp.where(is_high, high, jnp.where(step == 0, mid, zero)))
    return plain, moment


def split(value):
    coarse = value.astype(BF16)
    fine = (value - coarse.astype(F32)).astype(BF16)
    return coarse, fine


def low_half(shape):
    return lax.broadcasted_iota(jnp.int32, shape, len(shape) - 1) % 128 < NZ


def swap_half(value):
    return pltpu.roll(value, NZ, value.ndim - 1)


def scatter_product(lhs, depth_plain, depth_moment):
    rhs = jnp.concatenate([depth_plain, depth_moment], axis=1)
    rhs = jnp.concatenate(split(rhs), axis=0)
    coarse, fine = split(lhs)
    dims = (((1,), (1,)), ((), ()))
    return lax.dot_general(coarse, rhs, dims, preferred_element_type=F32) + lax.dot_general(
        fine, rhs, dims, preferred_element_type=F32
    )


def row_of(value, g):
    return value[g : g + 1, :]


def join_pairs(value, first, second):
    return jnp.concatenate([value[first : first + 1, :], value[second : second + 1, :]], axis=1)


def fold_pair(first, second):
    low = low_half(first.shape)
    return jnp.where(low, first, second) + swap_half(jnp.where(low, second, first))


def resident_living(count_ref, y):
    lane = 128 * (y // 2)
    counts = count_ref[:, lane : lane + 128]
    low = low_half(counts.shape)
    if y % 2 == 0:
        counts = jnp.where(low, counts, swap_half(counts))
    else:
        counts = jnp.where(low, swap_half(counts), counts)
    counts = jnp.concatenate([counts, counts], axis=0)
    row = lax.broadcasted_iota(jnp.int32, (8, 128), 0)
    lane_id = lax.broadcasted_iota(jnp.int32, (8, 128), 1)
    slot = 2 * (row // CX) + lane_id // NZ
    return (slot < counts).astype(F32)


def deposit_residents(res_ref, count_ref, terms_ref, total_ref, first, last):
    row = lax.broadcasted_iota(jnp.int32, (8, 128), 0)
    keep = row < CX
    for y in range(first, last):
        state = [res_ref[c, y] for c in range(16)]
        mass, carried, affine = deposit_terms(state, resident_living(count_ref, y))
        stored = [mass] + carried + affine
        for axis in range(3):
            stored += list(spline(state[axis]))
        for k, value in enumerate(stored):
            terms_ref[y, k] = value
    for ex in STEPS:
        sums = {}

        def finish_node(node):
            for c in range(4):
                value = (
                    sums.pop((node, c, 0))
                    + pltpu.roll(sums.pop((node, c, 1)), 1, 1)
                    + pltpu.roll(sums.pop((node, c, -1)), 127, 1)
                )
                value = jnp.where(keep, value + pltpu.roll(value, CX, 0), 0.0)
                if ex != 0:
                    value = pltpu.roll(value, ex % 8, 0)
                at = (node + 2) * 8
                total_ref[c, at : at + 8, :] += value

        for y in range(first, last):
            term = [terms_ref[y, k] for k in range(13)]
            weight_x = terms_ref[y, 13 + ex + 1]
            weight_y = [terms_ref[y, 16 + k] for k in range(3)]
            along = [term[0]]
            for i in range(3):
                value = term[1 + i]
                if ex != 0:
                    value = value + term[4 + 3 * i] if ex > 0 else value - term[4 + 3 * i]
                along.append(value)
            for ez in STEPS:
                weight = weight_x * terms_ref[y, 19 + ez + 1]
                for c in range(4):
                    value = along[c]
                    if c > 0 and ez != 0:
                        lift = term[4 + 3 * (c - 1) + 2]
                        value = value + lift if ez > 0 else value - lift
                    value = weight * value
                    parts = [value, value, value]
                    if c > 0:
                        lean = weight * term[4 + 3 * (c - 1) + 1]
                        parts = [value - lean, value, value + lean]
                    for ey in STEPS:
                        key = (y + ey, c, ez)
                        part = weight_y[ey + 1] * parts[ey + 1]
                        sums[key] = sums[key] + part if key in sums else part
            finish_node(y - 1)
        finish_node(last - 1)
        finish_node(last)


def edge_kernel(count_ref, res_ref, cells_ref, outbox_ref, corner_ref, face_cell_ref, corner_cell_ref,
                msg0_ref, msg1_ref, ahead_ref, total_ref, terms_ref, stage_ref):
    total_ref[...] = jnp.zeros_like(total_ref)

    def living_of(width, offset):
        slot = lax.broadcasted_iota(jnp.int32, (4, width), 1)
        row = lax.broadcasted_iota(jnp.int32, (4, width), 0)
        counts = jnp.where(
            row < 2,
            jnp.where(row == 0, count_ref[offset], count_ref[offset + 1]),
            jnp.where(row == 2, count_ref[offset + 2], count_ref[offset + 3]),
        )
        return slot < counts

    face_cells = jnp.where(living_of(MIG, 0), face_cell_ref[...], -1).astype(F32)
    corner_cells = jnp.where(living_of(CORNER, 4), corner_cell_ref[...], -1).astype(F32)

    faces = [outbox_ref[c] for c in range(16)]
    corners = [corner_ref[c] for c in range(16)]

    for c, (face, corner) in enumerate(zip(faces + [face_cells], corners + [corner_cells])):
        for side in range(2):
            pair = join_pairs(corner, side, side + 2)
            if c < 16:
                stage_ref[side, 48 + c : 49 + c, :] = face[2 + side : 3 + side, 0:128]
                stage_ref[side, 64 + c : 65 + c, :] = face[2 + side : 3 + side, 128:256]
                stage_ref[side, 80 + c : 81 + c, :] = pair
                ahead_ref[side, c : c + 1, :] = face[side : side + 1, 0:128]
                ahead_ref[side, 16 + c : 17 + c, :] = face[side : side + 1, 128:256]
            else:
                stage_ref[side, 96:97, :] = face[2 + side : 3 + side, 0:128]
                stage_ref[side, 97:98, :] = face[2 + side : 3 + side, 128:256]
                stage_ref[side, 98:99, :] = pair
                stage_ref[side, 99:104, :] = jnp.zeros((5, 128), F32)
                ahead_ref[side, 32:33, :] = face[side : side + 1, 0:128]
                ahead_ref[side, 33:34, :] = face[side : side + 1, 128:256]
                ahead_ref[side, 34:40, :] = jnp.zeros((6, 128), F32)

    def decode(cells):
        number = cells.astype(jnp.int32)
        living = (number >= 0).astype(F32)
        return living, number // (CY * NZ), (number // NZ) % CY, number % NZ

    def wide(face, corner):
        pairs = jnp.concatenate([join_pairs(corner, 0, 1), join_pairs(corner, 2, 3)], axis=0)
        return jnp.concatenate([face[0:2, :], pairs], axis=1)

    state = [wide(faces[c], corners[c]) for c in range(16)]
    living, _, cell_y, cell_z = decode(wide(face_cells, corner_cells))
    lane = lax.broadcasted_iota(jnp.int32, (2, WIDE), 1)
    cell_y = cell_y + jnp.where(lane < MIG, 2, jnp.where(lane < MIG + CORNER, 2 + CY, 2 - CY))
    mass, carried, affine = deposit_terms(state, living)
    weights = [spline(state[axis]) for axis in range(3)]
    for g in range(2):
        depth = placed(NZ, WIDE, row_of(cell_z, g), [row_of(w, g) for w in weights[2]])
        across, across_moment = placed(YP, WIDE, row_of(cell_y, g), [row_of(w, g) for w in weights[1]])
        lines = []
        zero = jnp.zeros((YP, WIDE), F32)
        for c in range(4):
            for e in STEPS:
                weight = row_of(weights[0][e + 1], g)
                if c == 0:
                    plain, moment = (weight * row_of(mass, g)) * across, zero
                else:
                    base = row_of(carried[c - 1], g) + e * row_of(affine[3 * (c - 1)], g)
                    plain = (weight * base) * across + (
                        weight * row_of(affine[3 * (c - 1) + 1], g)
                    ) * across_moment
                    moment = (weight * row_of(affine[3 * (c - 1) + 2], g)) * across
                lines.append(jnp.concatenate([plain, moment], axis=1))
        product = scatter_product(jnp.concatenate(lines, axis=0), *depth)
        for c in range(4):
            for e in STEPS:
                row = ((CX if g == 0 else -1) + e) % 8
                at = (3 * c + e + 1) * YP
                total_ref[c, pl.ds(row, YP, stride=8), :] += product[at : at + YP, :]

    state = [face[2:4, :] for face in faces]
    living, cell_x, _, cell_z = decode(face_cells[2:4, :])
    mass, carried, affine = deposit_terms(state, living)
    weights = [spline(state[axis]) for axis in range(3)]
    for g in range(2):
        depth = placed(NZ, MIG, row_of(cell_z, g), [row_of(w, g) for w in weights[2]])
        across, across_moment = placed(8, MIG, row_of(cell_x, g), [row_of(w, g) for w in weights[0]], 8)
        lines = []
        zero = jnp.zeros((8, MIG), F32)
        for c in range(4):
            for e in STEPS:
                weight = row_of(weights[1][e + 1], g)
                if c == 0:
                    plain, moment = (weight * row_of(mass, g)) * across, zero
                else:
                    base = row_of(carried[c - 1], g) + e * row_of(affine[3 * (c - 1) + 1], g)
                    plain = (weight * base) * across + (
                        weight * row_of(affine[3 * (c - 1)], g)
                    ) * across_moment
                    moment = (weight * row_of(affine[3 * (c - 1) + 2], g)) * across
                lines.append(jnp.concatenate([plain, moment], axis=1))
        product = scatter_product(jnp.concatenate(lines, axis=0), *depth)
        for c in range(4):
            for e in STEPS:
                at = ((CY if g == 0 else -1) + e + 2) * 8
                line = (3 * c + e + 1) * 8
                total_ref[c, at : at + 8, :] += product[line : line + 8, :]

    deposit_residents(res_ref, cells_ref, terms_ref, total_ref, 0, 2)
    deposit_residents(res_ref, cells_ref, terms_ref, total_ref, CY - 2, CY)

    for side in range(2):
        for pair in range(2):
            for j in range(3):
                at = ((CY + 1 + j) if side == 0 else j) * 8
                stage_ref[side, (3 * pair + j) * 8 : (3 * pair + j + 1) * 8, :] = fold_pair(
                    total_ref[2 * pair, at : at + 8, :], total_ref[2 * pair + 1, at : at + 8, :]
                )
    parity = lax.axis_index("gy") % 2
    msg0_ref[...] = stage_ref[parity]
    msg1_ref[...] = stage_ref[1 - parity]


def inner_kernel(res_ref, cells_ref, before_ref, grid_ref, total_ref, terms_ref):
    total_ref[...] = before_ref[...]
    deposit_residents(res_ref, cells_ref, terms_ref, total_ref, 2, CY - 2)
    for pair in range(2):
        for yy in range(YY):
            at = yy * 8
            grid_ref[pair, at : at + 8, :] = fold_pair(
                total_ref[2 * pair, at : at + 8, :], total_ref[2 * pair + 1, at : at + 8, :]
            )


def turn_kernel(grid_ref, in0_ref, in1_ref, ahead_ref, joined_ref, msg0_ref, msg1_ref, got_ref, stage_ref):
    parity = lax.axis_index("gy") % 2
    got_ref[parity] = in1_ref[...]
    got_ref[1 - parity] = in0_ref[...]
    joined_ref[...] = grid_ref[...]
    for pair in range(2):
        for j in range(3):
            line = (3 * pair + j) * 8
            for side, yy in ((0, 1 + j), (1, CY + j)):
                joined_ref[pair, yy * 8 : yy * 8 + 8, :] += got_ref[side, line : line + 8, :]
    low = low_half((16, 128))
    for side in range(2):
        for pair in range(2):
            for j in range(3):
                row = (3 + j) if side == 0 else (6 + j) % 8
                at = (3 * pair + j) * 18
                stage_ref[side, at : at + 18, :] = joined_ref[pair, pl.ds(8 + row, 18, stride=8), :]
        stage_ref[side, 108:112, :] = jnp.zeros((4, 128), F32)
        stage_ref[side, X_STATES : X_STATES + 32, :] = ahead_ref[side, 0:32, :]
        from_below, from_above = got_ref[0, 80:96, :], got_ref[1, 80:96, :]
        cell_below, cell_above = got_ref[0, 96:104, :], got_ref[1, 96:104, :]
        if side == 0:
            states = jnp.where(low, from_below, swap_half(from_above))
            cells = jnp.where(low[0:8], cell_below, swap_half(cell_above))
        else:
            states = jnp.where(low, swap_half(from_below), from_above)
            cells = jnp.where(low[0:8], swap_half(cell_below), cell_above)
        stage_ref[side, X_STATES + 32 : X_STATES + 48, :] = states
        stage_ref[side, X_STATES + 48 : X_STATES + 56, :] = jnp.zeros((8, 128), F32)
        stage_ref[side, X_STATES + 48 : X_STATES + 50, :] = ahead_ref[side, 32:34, :]
        stage_ref[side, X_STATES + 50 : X_STATES + 51, :] = cells[2:3, :]
    parity = lax.axis_index("gx") % 2
    msg0_ref[...] = stage_ref[parity]
    msg1_ref[...] = stage_ref[1 - parity]


def gather_product(nodes, depth_plain, depth_moment):
    low = low_half(nodes.shape)
    coarse = nodes.astype(BF16).astype(F32)
    lhs = jnp.where(low, coarse, nodes - coarse).astype(BF16)
    rhs = jnp.concatenate([depth_plain, depth_moment], axis=1)
    coarse, fine = split(rhs)
    dims = (((1,), (0,)), ((), ()))
    return lax.dot_general(
        lhs, jnp.concatenate([coarse, coarse], axis=0), dims, preferred_element_type=F32
    ) + lax.dot_general(lhs, jnp.concatenate([fine, fine], axis=0), dims, preferred_element_type=F32)


def contract(product, rows, width, normal, across, across_moment, normal_axis, across_axis):
    velocity, slopes = [], []
    for i in range(3):
        plain = [product[(3 * i + k) * rows : (3 * i + k + 1) * rows, 0:width] for k in range(3)]
        lifted = [
            product[(3 * i + k) * rows : (3 * i + k + 1) * rows, width : 2 * width] for k in range(3)
        ]
        low, mid, high = [normal[k] * plain[k] for k in range(3)]
        summed = low + mid + high
        stepped = high - low
        raised = normal[0] * lifted[0] + normal[1] * lifted[1] + normal[2] * lifted[2]
        velocity.append(jnp.sum(across * summed, axis=0, keepdims=True))
        slope = [None, None, jnp.sum(across * raised, axis=0, keepdims=True)]
        slope[normal_axis] = jnp.sum(across * stepped, axis=0, keepdims=True)
        slope[across_axis] = jnp.sum(across_moment * summed, axis=0, keepdims=True)
        slopes.append(slope)
    return velocity, slopes


def finished(state, living, velocity, slopes):
    out = [living * (state[k] + time_step * velocity[k]) for k in range(3)]
    out += [living * velocity[k] for k in range(3)]
    for i in range(3):
        out += [living * (4.0 * (slopes[i][k] - state[k] * velocity[i])) for k in range(3)]
    return out + [living * state[15]]


def last_kernel(res_ref, cells_ref, joined_ref, y0_ref, y1_ref, x0_ref, x1_ref,
                out_ref, face_out_ref, corner_out_ref, got_y_ref, got_x_ref, grid_ref, vel_ref, near_ref):
    parity = lax.axis_index("gy") % 2
    got_y_ref[parity] = y1_ref[...]
    got_y_ref[1 - parity] = y0_ref[...]
    parity = lax.axis_index("gx") % 2
    got_x_ref[parity] = x1_ref[...]
    got_x_ref[1 - parity] = x0_ref[...]

    grid_ref[...] = joined_ref[...]
    for side in range(2):
        for pair in range(2):
            for j in range(3):
                row = ((3 + j) if side == 0 else (6 + j) % 8) ^ 4
                at = (3 * pair + j) * 18
                grid_ref[pair, pl.ds(8 + row, 18, stride=8), :] += got_x_ref[side, at : at + 18, :]

    vel_ref[...] = jnp.zeros_like(vel_ref)
    low = low_half((8, 128))
    row = lax.broadcasted_iota(jnp.int32, (8, 128), 0)
    layer = lax.broadcasted_iota(jnp.int32, (8, 128), 1) % NZ
    inside = (layer > 0) & (layer < NZ - 1)
    upper = row < CX
    for yy in range(1, CY + 3):
        first = grid_ref[0, yy * 8 : yy * 8 + 8, :]
        second = grid_ref[1, yy * 8 : yy * 8 + 8, :]
        first_swap, second_swap = swap_half(first), swap_half(second)
        mass = jnp.maximum(jnp.where(low, first, first_swap), mass_floor)
        momentum = (
            jnp.where(low, first_swap, first),
            jnp.where(low, second, second_swap),
            jnp.where(low, second_swap, second),
        )
        for i in range(3):
            value = momentum[i] / mass
            if i == 2:
                value = value - time_step * gravity
            value = jnp.where(inside, value, 0.0)
            vel_ref[i, yy * 8 : yy * 8 + 8, :] = value
            for ex in STEPS:
                near = jnp.where(
                    upper,
                    pltpu.roll(value, (-ex) % 8, 0) if ex != 0 else value,
                    pltpu.roll(value, (CX - ex) % 8, 0),
                )
                near_ref[ex + 1, 1, i, yy - 1] = near
                near_ref[ex + 1, 0, i, yy - 1] = pltpu.roll(near, 1, 1)
                near_ref[ex + 1, 2, i, yy - 1] = pltpu.roll(near, 127, 1)

    for side in range(2):
        def wide_row(k):
            return jnp.concatenate([got_x_ref[side, a : a + 1, :] for a in k], axis=1)

        base = X_STATES
        state = [wide_row((base + c, base + 16 + c, base + 32 + c)) for c in range(16)]
        number = wide_row((base + 48, base + 49, base + 50)).astype(jnp.int32)
        living = (number >= 0).astype(F32)
        weights = [spline(state[axis]) for axis in range(3)]
        depth = placed(NZ, WIDE, number % NZ, weights[2])
        across, across_moment = placed(YP, WIDE, (number // NZ) % CY + 2, weights[1])
        lines = []
        for i in range(3):
            for e in STEPS:
                at = ((0 if side == 0 else CX - 1) + e) % 8
                lines.append(vel_ref[i, pl.ds(at, YP, stride=8), :])
        product = gather_product(jnp.concatenate(lines, axis=0), *depth)
        velocity, slopes = contract(product, YP, WIDE, weights[0], across, across_moment, 0, 1)
        for c, value in enumerate(finished(state, living, velocity, slopes)):
            face_out_ref[c, side : side + 1, :] = value[:, 0:MIG]
            corner_out_ref[c, 2 * side : 2 * side + 1, :] = value[:, MIG : MIG + CORNER]
            corner_out_ref[c, 2 * side + 1 : 2 * side + 2, :] = value[:, MIG + CORNER : WIDE]

    for side in range(2):
        def face_row(k):
            return jnp.concatenate([got_y_ref[side, a : a + 1, :] for a in k], axis=1)

        state = [face_row((48 + c, 64 + c)) for c in range(16)]
        number = face_row((96, 97)).astype(jnp.int32)
        living = (number >= 0).astype(F32)
        weights = [spline(state[axis]) for axis in range(3)]
        depth = placed(NZ, MIG, number % NZ, weights[2])
        across, across_moment = placed(8, MIG, jnp.maximum(number, 0) // (CY * NZ), weights[0], 8)
        lines = []
        for i in range(3):
            for e in STEPS:
                at = ((0 if side == 0 else CY - 1) + 2 + e) * 8
                lines.append(vel_ref[i, at : at + 8, :])
        product = gather_product(jnp.concatenate(lines, axis=0), *depth)
        velocity, slopes = contract(product, 8, MIG, weights[1], across, across_moment, 1, 0)
        for c, value in enumerate(finished(state, living, velocity, slopes)):
            face_out_ref[c, 2 + side : 3 + side, :] = value

    for y in range(CY):
        state = [res_ref[c, y] for c in range(16)]
        living = resident_living(cells_ref, y)
        weights = [spline(state[axis]) for axis in range(3)]
        velocity, slopes = [], []
        for i in range(3):
            by_x = []
            for kx in range(3):
                by_y = []
                for ky in range(3):
                    low_z, mid_z, high_z = [
                        weights[2][kz] * near_ref[kx, kz, i, y + ky] for kz in range(3)
                    ]
                    by_y.append((low_z + mid_z + high_z, high_z - low_z))
                low_y, mid_y, high_y = [weights[1][k] * by_y[k][0] for k in range(3)]
                raised = (
                    weights[1][0] * by_y[0][1] + weights[1][1] * by_y[1][1] + weights[1][2] * by_y[2][1]
                )
                by_x.append((low_y + mid_y + high_y, high_y - low_y, raised))
            low_x, mid_x, high_x = [weights[0][k] * by_x[k][0] for k in range(3)]
            velocity.append(low_x + mid_x + high_x)
            slope = [high_x - low_x]
            for part in (1, 2):
                slope.append(
                    weights[0][0] * by_x[0][part]
                    + weights[0][1] * by_x[1][part]
                    + weights[0][2] * by_x[2][part]
                )
            slopes.append(slope)
        for c, value in enumerate(finished(state, living, velocity, slopes)):
            out_ref[c, y] = value


def partner(index, phase, count):
    return (((index - phase) % count ^ 1) + phase) % count


def swapped(value, axis, phase):
    count = lax.axis_size(axis)
    return lax.ppermute(value, axis, [(i, partner(i, phase, count)) for i in range(count)])


VMEM = pl.BlockSpec(memory_space=pltpu.VMEM)
SMEM = pl.BlockSpec(memory_space=pltpu.SMEM)


def call(kernel, in_specs, out_shapes, scratch, flops):
    return pl.pallas_call(
        kernel,
        in_specs=in_specs,
        out_specs=[VMEM] * len(out_shapes),
        out_shape=[jax.ShapeDtypeStruct(shape, F32) for shape in out_shapes],
        scratch_shapes=[pltpu.VMEM(shape, F32) for shape in scratch],
        compiler_params=pltpu.CompilerParams(vmem_limit_bytes=24 * 1024 * 1024),
        cost_estimate=pl.CostEstimate(flops=flops, bytes_accessed=1 << 20, transcendentals=0),
    )


def body(residents, cell_count, outbox, corner_box, face_cell, corner_cell, mig_count):
    res = residents.reshape(16, CX, CY, 2, 128).transpose(0, 2, 3, 1, 4).reshape(16, CY, 8, 128)
    msg0, msg1, ahead, total = call(
        edge_kernel,
        [SMEM] + [VMEM] * 6,
        [(Y_ROWS, 128), (Y_ROWS, 128), (2, 40, 128), (4, YP * 8, 128)],
        [(CY, 22, 8, 128), (2, Y_ROWS, 128)],
        10_000_000,
    )(mig_count.reshape(8), res, cell_count, outbox, corner_box, face_cell, corner_cell)
    y1 = swapped(msg1, "gy", 1)
    y0 = swapped(msg0, "gy", 0)
    (grid,) = call(
        inner_kernel, [VMEM] * 3, [(2, YY * 8, 128)], [(4, YP * 8, 128), (CY, 22, 8, 128)], 10_000_000
    )(res, cell_count, total)
    joined, msg0, msg1 = call(
        turn_kernel,
        [VMEM] * 4,
        [(2, YY * 8, 128), (X_ROWS, 128), (X_ROWS, 128)],
        [(2, Y_ROWS, 128), (2, X_ROWS, 128)],
        1_000_000,
    )(grid, y0, y1, ahead)
    x1 = swapped(msg1, "gx", 1)
    x0 = swapped(msg0, "gx", 0)
    out, face_out, corner_out = call(
        last_kernel,
        [VMEM] * 7,
        [(16, CY, 8, 128), (16, 4, MIG), (16, 4, CORNER)],
        [
            (2, Y_ROWS, 128),
            (2, X_ROWS, 128),
            (2, YY * 8, 128),
            (3, YP * 8, 128),
            (3, 3, 3, CY + 2, 8, 128),
        ],
        10_000_000,
    )(res, cell_count, joined, y0, y1, x0, x1)
    out = out.reshape(16, CY, 2, CX, 128).transpose(0, 3, 1, 2, 4).reshape(16, CX, CY * 256)
    return out, face_out, corner_out


def solution(mesh):
    in_specs = (
        P(None, "gx", "gy"),
        P("gx", "gy"),
        P(None, "gx", "gy"),
        P(None, "gx", "gy"),
        P("gx", "gy"),
        P("gx", "gy"),
        P("gx", "gy"),
    )
    out_specs = (P(None, "gx", "gy"), P(None, "gx", "gy"), P(None, "gx", "gy"))
    return jax.shard_map(body, mesh=mesh, in_specs=in_specs, out_specs=out_specs, check_vma=False)
```

```python
import jax
import jax.numpy as jnp
from jax import lax
from jax.experimental import pallas as pl
from jax.experimental.pallas import tpu as pltpu
from jax.sharding import PartitionSpec as P

CX = 4
CY = 16
NZ = 64
MIG = 256
CORNER = 64
PAIR = 2 * CORNER
WIDE = MIG + PAIR
YY = 20
YP = 24
Y_ROWS = 104
X_ROWS = 168
X_STATES = 112
time_step = 0.1
gravity = 1.0
mass_floor = 0.5
STEPS = (-1, 0, 1)
F32 = jnp.float32
BF16 = jnp.bfloat16


def spline(offset):
    low = 0.5 - offset
    high = 0.5 + offset
    return (0.5 * (low * low), 0.75 - offset * offset, 0.5 * (high * high))


def deposit_terms(state, living):
    mass = state[15] * living
    affine = [mass * state[6 + j] for j in range(9)]
    carried = []
    for i in range(3):
        skew = affine[3 * i] * state[0] + affine[3 * i + 1] * state[1] + affine[3 * i + 2] * state[2]
        carried.append(mass * state[3 + i] - skew)
    return mass, carried, affine


def placed(rows, width, cell, weights, wrap=None, row=None):
    if row is None:
        row = lax.broadcasted_iota(jnp.int32, (rows, width), 0)
    step = row - cell
    if wrap is not None:
        step = jnp.where(step > wrap // 2, step - wrap, jnp.where(step < -wrap // 2, step + wrap, step))
    low, mid, high = weights
    zero = jnp.zeros((rows, width), F32)
    is_low, is_high = step == -1, step == 1
    moment = jnp.where(is_low, -low, jnp.where(is_high, high, zero))
    plain = jnp.where(is_low, low, jnp.where(is_high, high, jnp.where(step == 0, mid, zero)))
    return plain, moment


def split(value):
    coarse = value.astype(BF16)
    fine = (value - coarse.astype(F32)).astype(BF16)
    return coarse, fine


def low_half(shape):
    return lax.broadcasted_iota(jnp.int32, shape, len(shape) - 1) % 128 < NZ


def swap_half(value):
    return pltpu.roll(value, NZ, value.ndim - 1)


def scatter_product(lhs, depth_plain, depth_moment):
    rhs = jnp.concatenate([depth_plain, depth_moment], axis=1)
    rhs = jnp.concatenate(split(rhs), axis=0)
    coarse, fine = split(lhs)
    dims = (((1,), (1,)), ((), ()))
    return lax.dot_general(coarse, rhs, dims, preferred_element_type=F32) + lax.dot_general(
        fine, rhs, dims, preferred_element_type=F32
    )


def row_of(value, g):
    return value[g : g + 1, :]


def join_pairs(value, first, second):
    return jnp.concatenate([value[first : first + 1, :], value[second : second + 1, :]], axis=1)


def fold_pair(first, second):
    low = low_half(first.shape)
    return jnp.where(low, first, second) + swap_half(jnp.where(low, second, first))


def resident_living(count_ref, y):
    lane = 128 * (y // 2)
    counts = count_ref[:, lane : lane + 128]
    low = low_half(counts.shape)
    if y % 2 == 0:
        counts = jnp.where(low, counts, swap_half(counts))
    else:
        counts = jnp.where(low, swap_half(counts), counts)
    counts = jnp.concatenate([counts, counts], axis=0)
    row = lax.broadcasted_iota(jnp.int32, (8, 128), 0)
    lane_id = lax.broadcasted_iota(jnp.int32, (8, 128), 1)
    slot = 2 * (row // CX) + lane_id // NZ
    return (slot < counts).astype(F32)


def deposit_residents(res_ref, count_ref, terms_ref, total_ref, first, last, skip=0):
    row = lax.broadcasted_iota(jnp.int32, (8, 128), 0)
    keep = row < CX
    for y in range(first, last):
        state = [res_ref[c, y - skip] for c in range(16)]
        mass, carried, affine = deposit_terms(state, resident_living(count_ref, y))
        stored = [mass] + carried + affine
        for axis in range(3):
            stored += list(spline(state[axis]))
        for k, value in enumerate(stored):
            terms_ref[y, k] = value
    for ex in STEPS:
        sums = {}

        def finish_node(node):
            for c in range(4):
                value = (
                    sums.pop((node, c, 0))
                    + pltpu.roll(sums.pop((node, c, 1)), 1, 1)
                    + pltpu.roll(sums.pop((node, c, -1)), 127, 1)
                )
                value = jnp.where(keep, value + pltpu.roll(value, CX, 0), 0.0)
                if ex != 0:
                    value = pltpu.roll(value, ex % 8, 0)
                at = (node + 2) * 8
                total_ref[c, at : at + 8, :] += value

        for y in range(first, last):
            term = [terms_ref[y, k] for k in range(13)]
            weight_x = terms_ref[y, 13 + ex + 1]
            weight_y = [terms_ref[y, 16 + k] for k in range(3)]
            along = [term[0]]
            for i in range(3):
                value = term[1 + i]
                if ex != 0:
                    value = value + term[4 + 3 * i] if ex > 0 else value - term[4 + 3 * i]
                along.append(value)
            for ez in STEPS:
                weight = weight_x * terms_ref[y, 19 + ez + 1]
                for c in range(4):
                    value = along[c]
                    if c > 0 and ez != 0:
                        lift = term[4 + 3 * (c - 1) + 2]
                        value = value + lift if ez > 0 else value - lift
                    value = weight * value
                    parts = [value, value, value]
                    if c > 0:
                        lean = weight * term[4 + 3 * (c - 1) + 1]
                        parts = [value - lean, value, value + lean]
                    for ey in STEPS:
                        key = (y + ey, c, ez)
                        part = weight_y[ey + 1] * parts[ey + 1]
                        sums[key] = sums[key] + part if key in sums else part
            finish_node(y - 1)
        finish_node(last - 1)
        finish_node(last)


def decode(cells):
    number = cells.astype(jnp.int32)
    living = (number >= 0).astype(F32)
    return living, number // (CY * NZ), (number // NZ) % CY, number % NZ


def deposit_wide(state, cells, total_ref, row_nodes, chunks):
    rows = len(row_nodes)
    living, _, cell_y, cell_z = decode(cells)
    lane = lax.broadcasted_iota(jnp.int32, (2, WIDE), 1)
    cell_y = cell_y + jnp.where(lane < MIG, 2, jnp.where(lane < MIG + CORNER, 2 + CY, 2 - CY))
    mass, carried, affine = deposit_terms(state, living)
    weights = [spline(state[axis]) for axis in range(3)]
    row = lax.broadcasted_iota(jnp.int32, (rows, WIDE), 0)
    node = row
    for k in range(rows):
        if k == 0:
            node = row + row_nodes[0]
        elif row_nodes[k] != row_nodes[k - 1] + 1:
            node = jnp.where(row >= k, row + (row_nodes[k] - k), node)
    for g in range(2):
        depth = placed(NZ, WIDE, row_of(cell_z, g), [row_of(w, g) for w in weights[2]])
        across, across_moment = placed(
            rows, WIDE, row_of(cell_y, g), [row_of(w, g) for w in weights[1]], row=node
        )
        lines = []
        zero = jnp.zeros((rows, WIDE), F32)
        for c in range(4):
            for e in STEPS:
                weight = row_of(weights[0][e + 1], g)
                if c == 0:
                    plain, moment = (weight * row_of(mass, g)) * across, zero
                else:
                    base = row_of(carried[c - 1], g) + e * row_of(affine[3 * (c - 1)], g)
                    plain = (weight * base) * across + (
                        weight * row_of(affine[3 * (c - 1) + 1], g)
                    ) * across_moment
                    moment = (weight * row_of(affine[3 * (c - 1) + 2], g)) * across
                lines.append(jnp.concatenate([plain, moment], axis=1))
        product = scatter_product(jnp.concatenate(lines, axis=0), *depth)
        for c in range(4):
            for e in STEPS:
                row = ((CX if g == 0 else -1) + e) % 8
                for start, count in chunks:
                    at = (3 * c + e + 1) * rows + start
                    total_ref[c, pl.ds(row_nodes[start] * 8 + row, count, stride=8), :] += product[
                        at : at + count, :
                    ]


def edge_kernel(count_hbm, res_hbm, cells_hbm, outbox_hbm, corner_hbm, face_cell_hbm, corner_cell_hbm,
                msg0_ref, msg1_ref, ahead_ref, total_ref, wide_ref,
                terms_ref, stage_ref, res_ref, cells_ref, outbox_ref, corner_ref, face_cell_ref,
                corner_cell_ref, count_ref, sems):
    copies = [
        pltpu.make_async_copy(source, target, sems.at[k])
        for k, (source, target) in enumerate(
            [
                (count_hbm, count_ref),
                (face_cell_hbm, face_cell_ref),
                (corner_cell_hbm, corner_cell_ref),
                (outbox_hbm, outbox_ref),
                (corner_hbm, corner_ref),
                (cells_hbm, cells_ref),
                (res_hbm.at[:, 0:2], res_ref.at[:, 0:2]),
                (res_hbm.at[:, CY - 2 : CY], res_ref.at[:, 2:4]),
            ]
        )
    ]
    for copy in copies:
        copy.start()
    total_ref[...] = jnp.zeros_like(total_ref)
    for copy in copies[0:5]:
        copy.wait()

    def living_of(width, offset):
        slot = lax.broadcasted_iota(jnp.int32, (4, width), 1)
        row = lax.broadcasted_iota(jnp.int32, (4, width), 0)
        counts = jnp.where(
            row < 2,
            jnp.where(row == 0, count_ref[offset], count_ref[offset + 1]),
            jnp.where(row == 2, count_ref[offset + 2], count_ref[offset + 3]),
        )
        return slot < counts

    face_cells = jnp.where(living_of(MIG, 0), face_cell_ref[...], -1).astype(F32)
    corner_cells = jnp.where(living_of(CORNER, 4), corner_cell_ref[...], -1).astype(F32)

    faces = [outbox_ref[c] for c in range(16)]
    corners = [corner_ref[c] for c in range(16)]

    for c, (face, corner) in enumerate(zip(faces + [face_cells], corners + [corner_cells])):
        for side in range(2):
            pair = join_pairs(corner, side, side + 2)
            if c < 16:
                stage_ref[side, 48 + c : 49 + c, :] = face[2 + side : 3 + side, 0:128]
                stage_ref[side, 64 + c : 65 + c, :] = face[2 + side : 3 + side, 128:256]
                stage_ref[side, 80 + c : 81 + c, :] = pair
                ahead_ref[side, c : c + 1, :] = face[side : side + 1, 0:128]
                ahead_ref[side, 16 + c : 17 + c, :] = face[side : side + 1, 128:256]
            else:
                stage_ref[side, 96:97, :] = face[2 + side : 3 + side, 0:128]
                stage_ref[side, 97:98, :] = face[2 + side : 3 + side, 128:256]
                stage_ref[side, 98:99, :] = pair
                stage_ref[side, 99:104, :] = jnp.zeros((5, 128), F32)
                ahead_ref[side, 32:33, :] = face[side : side + 1, 0:128]
                ahead_ref[side, 33:34, :] = face[side : side + 1, 128:256]
                ahead_ref[side, 34:40, :] = jnp.zeros((6, 128), F32)

    def wide(face, corner):
        pairs = jnp.concatenate([join_pairs(corner, 0, 1), join_pairs(corner, 2, 3)], axis=0)
        return jnp.concatenate([face[0:2, :], pairs], axis=1)

    state = [wide(faces[c], corners[c]) for c in range(16)] + [wide(face_cells, corner_cells)]
    for c, value in enumerate(state):
        wide_ref[c] = value
    deposit_wide(
        state[:16], state[16], total_ref, [0, 1, 2, 17, 18, 19, 100, 101], [(0, 3), (3, 3)]
    )

    state = [face[2:4, :] for face in faces]
    living, cell_x, _, cell_z = decode(face_cells[2:4, :])
    mass, carried, affine = deposit_terms(state, living)
    weights = [spline(state[axis]) for axis in range(3)]
    for g in range(2):
        depth = placed(NZ, MIG, row_of(cell_z, g), [row_of(w, g) for w in weights[2]])
        across, across_moment = placed(8, MIG, row_of(cell_x, g), [row_of(w, g) for w in weights[0]], 8)
        lines = []
        zero = jnp.zeros((8, MIG), F32)
        for c in range(4):
            for e in STEPS:
                weight = row_of(weights[1][e + 1], g)
                if c == 0:
                    plain, moment = (weight * row_of(mass, g)) * across, zero
                else:
                    base = row_of(carried[c - 1], g) + e * row_of(affine[3 * (c - 1) + 1], g)
                    plain = (weight * base) * across + (
                        weight * row_of(affine[3 * (c - 1)], g)
                    ) * across_moment
                    moment = (weight * row_of(affine[3 * (c - 1) + 2], g)) * across
                lines.append(jnp.concatenate([plain, moment], axis=1))
        product = scatter_product(jnp.concatenate(lines, axis=0), *depth)
        for c in range(4):
            for e in STEPS:
                at = ((CY if g == 0 else -1) + e + 2) * 8
                line = (3 * c + e + 1) * 8
                total_ref[c, at : at + 8, :] += product[line : line + 8, :]

    for copy in copies[5:]:
        copy.wait()
    deposit_residents(res_ref, cells_ref, terms_ref, total_ref, 0, 2)
    deposit_residents(res_ref, cells_ref, terms_ref, total_ref, CY - 2, CY, CY - 4)

    for side in range(2):
        for pair in range(2):
            for j in range(3):
                at = ((CY + 1 + j) if side == 0 else j) * 8
                stage_ref[side, (3 * pair + j) * 8 : (3 * pair + j + 1) * 8, :] = fold_pair(
                    total_ref[2 * pair, at : at + 8, :], total_ref[2 * pair + 1, at : at + 8, :]
                )
    parity = lax.axis_index("gy") % 2
    msg0_ref[...] = stage_ref[parity]
    msg1_ref[...] = stage_ref[1 - parity]


def inner_kernel(res_ref, cells_ref, before_ref, wide_ref, grid_ref, total_ref, terms_ref):
    total_ref[...] = before_ref[...]
    deposit_wide(
        [wide_ref[c] for c in range(16)], wide_ref[16], total_ref, list(range(3, 19)), [(0, 14)]
    )
    deposit_residents(res_ref, cells_ref, terms_ref, total_ref, 2, CY - 2)
    for pair in range(2):
        for yy in range(YY):
            at = yy * 8
            grid_ref[pair, at : at + 8, :] = fold_pair(
                total_ref[2 * pair, at : at + 8, :], total_ref[2 * pair + 1, at : at + 8, :]
            )


def turn_kernel(grid_ref, in1_ref, in0_ref, ahead_ref, joined_ref, msg0_ref, msg1_ref, got_ref, stage_ref):
    parity = lax.axis_index("gy") % 2
    got_ref[parity] = in1_ref[...]
    got_ref[1 - parity] = in0_ref[...]
    joined_ref[...] = grid_ref[...]
    for pair in range(2):
        for j in range(3):
            line = (3 * pair + j) * 8
            for side, yy in ((0, 1 + j), (1, CY + j)):
                joined_ref[pair, yy * 8 : yy * 8 + 8, :] += got_ref[side, line : line + 8, :]
    low = low_half((16, 128))
    for side in range(2):
        for pair in range(2):
            for j in range(3):
                row = (3 + j) if side == 0 else (6 + j) % 8
                at = (3 * pair + j) * 18
                stage_ref[side, at : at + 18, :] = joined_ref[pair, pl.ds(8 + row, 18, stride=8), :]
        stage_ref[side, 108:112, :] = jnp.zeros((4, 128), F32)
        stage_ref[side, X_STATES : X_STATES + 32, :] = ahead_ref[side, 0:32, :]
        from_below, from_above = got_ref[0, 80:96, :], got_ref[1, 80:96, :]
        cell_below, cell_above = got_ref[0, 96:104, :], got_ref[1, 96:104, :]
        if side == 0:
            states = jnp.where(low, from_below, swap_half(from_above))
            cells = jnp.where(low[0:8], cell_below, swap_half(cell_above))
        else:
            states = jnp.where(low, swap_half(from_below), from_above)
            cells = jnp.where(low[0:8], swap_half(cell_below), cell_above)
        stage_ref[side, X_STATES + 32 : X_STATES + 48, :] = states
        stage_ref[side, X_STATES + 48 : X_STATES + 56, :] = jnp.zeros((8, 128), F32)
        stage_ref[side, X_STATES + 48 : X_STATES + 50, :] = ahead_ref[side, 32:34, :]
        stage_ref[side, X_STATES + 50 : X_STATES + 51, :] = cells[2:3, :]
    parity = lax.axis_index("gx") % 2
    msg0_ref[...] = stage_ref[parity]
    msg1_ref[...] = stage_ref[1 - parity]


def gather_product(nodes, depth_plain, depth_moment):
    low = low_half(nodes.shape)
    coarse = nodes.astype(BF16).astype(F32)
    lhs = jnp.where(low, coarse, nodes - coarse).astype(BF16)
    rhs = jnp.concatenate([depth_plain, depth_moment], axis=1)
    coarse, fine = split(rhs)
    dims = (((1,), (0,)), ((), ()))
    return lax.dot_general(
        lhs, jnp.concatenate([coarse, coarse], axis=0), dims, preferred_element_type=F32
    ) + lax.dot_general(lhs, jnp.concatenate([fine, fine], axis=0), dims, preferred_element_type=F32)


def contract(product, rows, width, normal, across, across_moment, normal_axis, across_axis):
    velocity, slopes = [], []
    for i in range(3):
        plain = [product[(3 * i + k) * rows : (3 * i + k + 1) * rows, 0:width] for k in range(3)]
        lifted = [
            product[(3 * i + k) * rows : (3 * i + k + 1) * rows, width : 2 * width] for k in range(3)
        ]
        low, mid, high = [normal[k] * plain[k] for k in range(3)]
        summed = low + mid + high
        stepped = high - low
        raised = normal[0] * lifted[0] + normal[1] * lifted[1] + normal[2] * lifted[2]
        velocity.append(jnp.sum(across * summed, axis=0, keepdims=True))
        slope = [None, None, jnp.sum(across * raised, axis=0, keepdims=True)]
        slope[normal_axis] = jnp.sum(across * stepped, axis=0, keepdims=True)
        slope[across_axis] = jnp.sum(across_moment * summed, axis=0, keepdims=True)
        slopes.append(slope)
    return velocity, slopes


def finished(state, living, velocity, slopes):
    out = [living * (state[k] + time_step * velocity[k]) for k in range(3)]
    out += [living * velocity[k] for k in range(3)]
    for i in range(3):
        out += [living * (4.0 * (slopes[i][k] - state[k] * velocity[i])) for k in range(3)]
    return out + [living * state[15]]


def last_kernel(res_ref, cells_ref, joined_ref, y1_ref, y0_ref, x1_ref, x0_ref,
                out_hbm, face_out_hbm, corner_out_hbm, got_y_ref, got_x_ref, grid_ref, vel_ref, near_ref,
                out_ref, face_out_ref, corner_out_ref, sems):
    parity = lax.axis_index("gy") % 2
    got_y_ref[parity] = y1_ref[...]
    got_y_ref[1 - parity] = y0_ref[...]
    parity = lax.axis_index("gx") % 2
    got_x_ref[parity] = x1_ref[...]
    got_x_ref[1 - parity] = x0_ref[...]

    grid_ref[...] = joined_ref[...]
    for side in range(2):
        for pair in range(2):
            for j in range(3):
                row = ((3 + j) if side == 0 else (6 + j) % 8) ^ 4
                at = (3 * pair + j) * 18
                grid_ref[pair, pl.ds(8 + row, 18, stride=8), :] += got_x_ref[side, at : at + 18, :]

    vel_ref[...] = jnp.zeros_like(vel_ref)
    low = low_half((8, 128))
    row = lax.broadcasted_iota(jnp.int32, (8, 128), 0)
    layer = lax.broadcasted_iota(jnp.int32, (8, 128), 1) % NZ
    inside = (layer > 0) & (layer < NZ - 1)
    upper = row < CX
    for yy in range(1, CY + 3):
        first = grid_ref[0, yy * 8 : yy * 8 + 8, :]
        second = grid_ref[1, yy * 8 : yy * 8 + 8, :]
        first_swap, second_swap = swap_half(first), swap_half(second)
        mass = jnp.maximum(jnp.where(low, first, first_swap), mass_floor)
        momentum = (
            jnp.where(low, first_swap, first),
            jnp.where(low, second, second_swap),
            jnp.where(low, second_swap, second),
        )
        for i in range(3):
            value = momentum[i] / mass
            if i == 2:
                value = value - time_step * gravity
            value = jnp.where(inside, value, 0.0)
            vel_ref[i, yy * 8 : yy * 8 + 8, :] = value
            for ex in STEPS:
                near = jnp.where(
                    upper,
                    pltpu.roll(value, (-ex) % 8, 0) if ex != 0 else value,
                    pltpu.roll(value, (CX - ex) % 8, 0),
                )
                near_ref[ex + 1, 1, i, yy - 1] = near
                near_ref[ex + 1, 0, i, yy - 1] = pltpu.roll(near, 1, 1)
                near_ref[ex + 1, 2, i, yy - 1] = pltpu.roll(near, 127, 1)

    copies = []
    for y in range(CY):
        state = [res_ref[c, y] for c in range(16)]
        living = resident_living(cells_ref, y)
        weights = [spline(state[axis]) for axis in range(3)]
        velocity, slopes = [], []
        for i in range(3):
            by_x = []
            for kx in range(3):
                by_y = []
                for ky in range(3):
                    low_z, mid_z, high_z = [
                        weights[2][kz] * near_ref[kx, kz, i, y + ky] for kz in range(3)
                    ]
                    by_y.append((low_z + mid_z + high_z, high_z - low_z))
                low_y, mid_y, high_y = [weights[1][k] * by_y[k][0] for k in range(3)]
                raised = (
                    weights[1][0] * by_y[0][1] + weights[1][1] * by_y[1][1] + weights[1][2] * by_y[2][1]
                )
                by_x.append((low_y + mid_y + high_y, high_y - low_y, raised))
            low_x, mid_x, high_x = [weights[0][k] * by_x[k][0] for k in range(3)]
            velocity.append(low_x + mid_x + high_x)
            slope = [high_x - low_x]
            for part in (1, 2):
                slope.append(
                    weights[0][0] * by_x[0][part]
                    + weights[0][1] * by_x[1][part]
                    + weights[0][2] * by_x[2][part]
                )
            slopes.append(slope)
        for c, value in enumerate(finished(state, living, velocity, slopes)):
            out_ref[c, y] = value
        if y % 4 == 3:
            copies.append(
                pltpu.make_async_copy(
                    out_ref.at[:, y - 3 : y + 1], out_hbm.at[:, y - 3 : y + 1], sems.at[y // 4]
                )
            )
            copies[-1].start()

    for side in range(2):
        def wide_row(k):
            return jnp.concatenate([got_x_ref[side, a : a + 1, :] for a in k], axis=1)

        base = X_STATES
        state = [wide_row((base + c, base + 16 + c, base + 32 + c)) for c in range(16)]
        number = wide_row((base + 48, base + 49, base + 50)).astype(jnp.int32)
        living = (number >= 0).astype(F32)
        weights = [spline(state[axis]) for axis in range(3)]
        depth = placed(NZ, WIDE, number % NZ, weights[2])
        across, across_moment = placed(YP, WIDE, (number // NZ) % CY + 2, weights[1])
        lines = []
        for i in range(3):
            for e in STEPS:
                at = ((0 if side == 0 else CX - 1) + e) % 8
                lines.append(vel_ref[i, pl.ds(at, YP, stride=8), :])
        product = gather_product(jnp.concatenate(lines, axis=0), *depth)
        velocity, slopes = contract(product, YP, WIDE, weights[0], across, across_moment, 0, 1)
        for c, value in enumerate(finished(state, living, velocity, slopes)):
            face_out_ref[c, side : side + 1, :] = value[:, 0:MIG]
            corner_out_ref[c, 2 * side : 2 * side + 1, :] = value[:, MIG : MIG + CORNER]
            corner_out_ref[c, 2 * side + 1 : 2 * side + 2, :] = value[:, MIG + CORNER : WIDE]

    for side in range(2):
        def face_row(k):
            return jnp.concatenate([got_y_ref[side, a : a + 1, :] for a in k], axis=1)

        state = [face_row((48 + c, 64 + c)) for c in range(16)]
        number = face_row((96, 97)).astype(jnp.int32)
        living = (number >= 0).astype(F32)
        weights = [spline(state[axis]) for axis in range(3)]
        depth = placed(NZ, MIG, number % NZ, weights[2])
        across, across_moment = placed(8, MIG, jnp.maximum(number, 0) // (CY * NZ), weights[0], 8)
        lines = []
        for i in range(3):
            for e in STEPS:
                at = ((0 if side == 0 else CY - 1) + 2 + e) * 8
                lines.append(vel_ref[i, at : at + 8, :])
        product = gather_product(jnp.concatenate(lines, axis=0), *depth)
        velocity, slopes = contract(product, 8, MIG, weights[1], across, across_moment, 1, 0)
        for c, value in enumerate(finished(state, living, velocity, slopes)):
            face_out_ref[c, 2 + side : 3 + side, :] = value

    copies.append(pltpu.make_async_copy(face_out_ref, face_out_hbm, sems.at[4]))
    copies.append(pltpu.make_async_copy(corner_out_ref, corner_out_hbm, sems.at[5]))
    for copy in copies[-2:]:
        copy.start()
    for copy in copies:
        copy.wait()


def partner(index, phase, count):
    return (((index - phase) % count ^ 1) + phase) % count


def swapped(value, axis, phase):
    count = lax.axis_size(axis)
    return lax.ppermute(value, axis, [(i, partner(i, phase, count)) for i in range(count)])


VMEM = pl.BlockSpec(memory_space=pltpu.VMEM)
HBM = pl.BlockSpec(memory_space=pltpu.HBM)


def scratch(shape, dtype=F32):
    return pltpu.VMEM(shape, dtype)


def call(kernel, in_specs, out_spec, out_shapes, scratch_shapes, flops, limit=24):
    return pl.pallas_call(
        kernel,
        in_specs=in_specs,
        out_specs=[out_spec] * len(out_shapes),
        out_shape=[jax.ShapeDtypeStruct(shape, F32) for shape in out_shapes],
        scratch_shapes=scratch_shapes,
        compiler_params=pltpu.CompilerParams(vmem_limit_bytes=limit * 1024 * 1024),
        cost_estimate=pl.CostEstimate(flops=flops, bytes_accessed=1 << 20, transcendentals=0),
    )


def body(residents, cell_count, outbox, corner_box, face_cell, corner_cell, mig_count):
    res = residents.reshape(16, CX, CY, 2, 128).transpose(0, 2, 3, 1, 4).reshape(16, CY, 8, 128)
    msg0, msg1, ahead, total, wide = call(
        edge_kernel,
        [HBM] * 7,
        VMEM,
        [(Y_ROWS, 128), (Y_ROWS, 128), (2, 40, 128), (4, YP * 8, 128), (17, 2, WIDE)],
        [
            scratch((CY, 22, 8, 128)),
            scratch((2, Y_ROWS, 128)),
            scratch((16, 4, 8, 128)),
            scratch((CX, CY * NZ), jnp.int32),
            scratch((16, 4, MIG)),
            scratch((16, 4, CORNER)),
            scratch((4, MIG), jnp.int32),
            scratch((4, CORNER), jnp.int32),
            pltpu.SMEM((8,), jnp.int32),
            pltpu.SemaphoreType.DMA((8,)),
        ],
        10_000_000,
        62,
    )(mig_count.reshape(8), res, cell_count, outbox, corner_box, face_cell, corner_cell)
    y0 = swapped(msg0, "gy", 0)
    y1 = swapped(msg1, "gy", 1)
    (grid,) = call(
        inner_kernel,
        [VMEM] * 4,
        VMEM,
        [(2, YY * 8, 128)],
        [scratch((4, YP * 8, 128)), scratch((CY, 22, 8, 128))],
        10_000_000,
    )(res, cell_count, total, wide)
    joined, msg0, msg1 = call(
        turn_kernel,
        [VMEM] * 4,
        VMEM,
        [(2, YY * 8, 128), (X_ROWS, 128), (X_ROWS, 128)],
        [scratch((2, Y_ROWS, 128)), scratch((2, X_ROWS, 128))],
        1_000_000,
    )(grid, y1, y0, ahead)
    x0 = swapped(msg0, "gx", 0)
    x1 = swapped(msg1, "gx", 1)
    out, face_out, corner_out = call(
        last_kernel,
        [VMEM] * 7,
        HBM,
        [(16, CY, 8, 128), (16, 4, MIG), (16, 4, CORNER)],
        [
            scratch((2, Y_ROWS, 128)),
            scratch((2, X_ROWS, 128)),
            scratch((2, YY * 8, 128)),
            scratch((3, YP * 8, 128)),
            scratch((3, 3, 3, CY + 2, 8, 128)),
            scratch((16, CY, 8, 128)),
            scratch((16, 4, MIG)),
            scratch((16, 4, CORNER)),
            pltpu.SemaphoreType.DMA((6,)),
        ],
        10_000_000,
    )(res, cell_count, joined, y1, y0, x1, x0)
    out = out.reshape(16, CY, 2, CX, 128).transpose(0, 3, 1, 2, 4).reshape(16, CX, CY * 256)
    return out, face_out, corner_out


def solution(mesh):
    in_specs = (
        P(None, "gx", "gy"),
        P("gx", "gy"),
        P(None, "gx", "gy"),
        P(None, "gx", "gy"),
        P("gx", "gy"),
        P("gx", "gy"),
        P("gx", "gy"),
    )
    out_specs = (P(None, "gx", "gy"), P(None, "gx", "gy"), P(None, "gx", "gy"))
    return jax.shard_map(body, mesh=mesh, in_specs=in_specs, out_specs=out_specs, check_vma=False)
```

```python
import jax
import jax.numpy as jnp
from jax import lax
from jax.experimental import pallas as pl
from jax.experimental.pallas import tpu as pltpu
from jax.sharding import PartitionSpec as P

CX = 4
CY = 16
NZ = 64
MIG = 256
CORNER = 64
PAIR = 2 * CORNER
WIDE = MIG + PAIR
YY = 20
YP = 24
Y_ROWS = 104
X_ROWS = 168
X_STATES = 112
time_step = 0.1
gravity = 1.0
mass_floor = 0.5
STEPS = (-1, 0, 1)
F32 = jnp.float32
BF16 = jnp.bfloat16


def spline(offset):
    low = 0.5 - offset
    high = 0.5 + offset
    return (0.5 * (low * low), 0.75 - offset * offset, 0.5 * (high * high))


def deposit_terms(state, living):
    mass = state[15] * living
    affine = [mass * state[6 + j] for j in range(9)]
    carried = []
    for i in range(3):
        skew = affine[3 * i] * state[0] + affine[3 * i + 1] * state[1] + affine[3 * i + 2] * state[2]
        carried.append(mass * state[3 + i] - skew)
    return mass, carried, affine


def placed(rows, width, cell, weights, wrap=None, row=None):
    if row is None:
        row = lax.broadcasted_iota(jnp.int32, (rows, width), 0)
    step = row - cell
    if wrap is not None:
        step = jnp.where(step > wrap // 2, step - wrap, jnp.where(step < -wrap // 2, step + wrap, step))
    low, mid, high = weights
    zero = jnp.zeros((rows, width), F32)
    is_low, is_high = step == -1, step == 1
    moment = jnp.where(is_low, -low, jnp.where(is_high, high, zero))
    plain = jnp.where(is_low, low, jnp.where(is_high, high, jnp.where(step == 0, mid, zero)))
    return plain, moment


def split(value):
    coarse = value.astype(BF16)
    fine = (value - coarse.astype(F32)).astype(BF16)
    return coarse, fine


def low_half(shape):
    return lax.broadcasted_iota(jnp.int32, shape, len(shape) - 1) % 128 < NZ


def swap_half(value):
    return pltpu.roll(value, NZ, value.ndim - 1)


def scatter_product(lhs, depth_plain, depth_moment):
    rhs = jnp.concatenate([depth_plain, depth_moment], axis=1)
    rhs = jnp.concatenate(split(rhs), axis=0)
    rows = lhs.shape[0]
    product = lax.dot_general(
        jnp.concatenate(split(lhs), axis=0), rhs, (((1,), (1,)), ((), ())), preferred_element_type=F32
    )
    return product[0:rows] + product[rows : 2 * rows]


def row_of(value, g):
    return value[g : g + 1, :]


def join_pairs(value, first, second):
    return jnp.concatenate([value[first : first + 1, :], value[second : second + 1, :]], axis=1)


def fold_pair(first, second):
    low = low_half(first.shape)
    return jnp.where(low, first, second) + swap_half(jnp.where(low, second, first))


def resident_living(count_ref, y):
    lane = 128 * (y // 2)
    counts = count_ref[:, lane : lane + 128]
    low = low_half(counts.shape)
    if y % 2 == 0:
        counts = jnp.where(low, counts, swap_half(counts))
    else:
        counts = jnp.where(low, swap_half(counts), counts)
    counts = jnp.concatenate([counts, counts], axis=0)
    row = lax.broadcasted_iota(jnp.int32, (8, 128), 0)
    lane_id = lax.broadcasted_iota(jnp.int32, (8, 128), 1)
    slot = 2 * (row // CX) + lane_id // NZ
    return (slot < counts).astype(F32)


def deposit_residents(res_ref, count_ref, terms_ref, total_ref, first, last):
    row = lax.broadcasted_iota(jnp.int32, (8, 128), 0)
    keep = row < CX
    for y in range(first, last):
        state = [res_ref[c, y] for c in range(16)]
        mass, carried, affine = deposit_terms(state, resident_living(count_ref, y))
        stored = [mass] + carried + affine
        for axis in range(3):
            stored += list(spline(state[axis]))
        for k, value in enumerate(stored):
            terms_ref[y, k] = value
    for ex in STEPS:
        sums = {}

        def finish_node(node):
            for c in range(4):
                value = (
                    sums.pop((node, c, 0))
                    + pltpu.roll(sums.pop((node, c, 1)), 1, 1)
                    + pltpu.roll(sums.pop((node, c, -1)), 127, 1)
                )
                value = jnp.where(keep, value + pltpu.roll(value, CX, 0), 0.0)
                if ex != 0:
                    value = pltpu.roll(value, ex % 8, 0)
                at = (node + 2) * 8
                total_ref[c, at : at + 8, :] += value

        for y in range(first, last):
            term = [terms_ref[y, k] for k in range(13)]
            weight_x = terms_ref[y, 13 + ex + 1]
            weight_y = [terms_ref[y, 16 + k] for k in range(3)]
            along = [term[0]]
            for i in range(3):
                value = term[1 + i]
                if ex != 0:
                    value = value + term[4 + 3 * i] if ex > 0 else value - term[4 + 3 * i]
                along.append(value)
            for ez in STEPS:
                weight = weight_x * terms_ref[y, 19 + ez + 1]
                for c in range(4):
                    value = along[c]
                    if c > 0 and ez != 0:
                        lift = term[4 + 3 * (c - 1) + 2]
                        value = value + lift if ez > 0 else value - lift
                    value = weight * value
                    parts = [value, value, value]
                    if c > 0:
                        lean = weight * term[4 + 3 * (c - 1) + 1]
                        parts = [value - lean, value, value + lean]
                    for ey in STEPS:
                        key = (y + ey, c, ez)
                        part = weight_y[ey + 1] * parts[ey + 1]
                        sums[key] = sums[key] + part if key in sums else part
            finish_node(y - 1)
        finish_node(last - 1)
        finish_node(last)


def decode(cells):
    number = cells.astype(jnp.int32)
    living = (number >= 0).astype(F32)
    return living, number // (CY * NZ), (number // NZ) % CY, number % NZ


def deposit_wide(state, cells, total_ref, row_nodes, chunks):
    rows = len(row_nodes)
    living, _, cell_y, cell_z = decode(cells)
    lane = lax.broadcasted_iota(jnp.int32, (2, WIDE), 1)
    cell_y = cell_y + jnp.where(lane < MIG, 2, jnp.where(lane < MIG + CORNER, 2 + CY, 2 - CY))
    mass, carried, affine = deposit_terms(state, living)
    weights = [spline(state[axis]) for axis in range(3)]
    row = lax.broadcasted_iota(jnp.int32, (rows, WIDE), 0)
    node = row
    for k in range(rows):
        if k == 0:
            node = row + row_nodes[0]
        elif row_nodes[k] != row_nodes[k - 1] + 1:
            node = jnp.where(row >= k, row + (row_nodes[k] - k), node)
    for g in range(2):
        depth = placed(NZ, WIDE, row_of(cell_z, g), [row_of(w, g) for w in weights[2]])
        across, across_moment = placed(
            rows, WIDE, row_of(cell_y, g), [row_of(w, g) for w in weights[1]], row=node
        )
        lines = []
        zero = jnp.zeros((rows, WIDE), F32)
        for c in range(4):
            for e in STEPS:
                weight = row_of(weights[0][e + 1], g)
                if c == 0:
                    plain, moment = (weight * row_of(mass, g)) * across, zero
                else:
                    base = row_of(carried[c - 1], g) + e * row_of(affine[3 * (c - 1)], g)
                    plain = (weight * base) * across + (
                        weight * row_of(affine[3 * (c - 1) + 1], g)
                    ) * across_moment
                    moment = (weight * row_of(affine[3 * (c - 1) + 2], g)) * across
                lines.append(jnp.concatenate([plain, moment], axis=1))
        product = scatter_product(jnp.concatenate(lines, axis=0), *depth)
        for c in range(4):
            for e in STEPS:
                row = ((CX if g == 0 else -1) + e) % 8
                for start, count in chunks:
                    at = (3 * c + e + 1) * rows + start
                    total_ref[c, pl.ds(row_nodes[start] * 8 + row, count, stride=8), :] += product[
                        at : at + count, :
                    ]


def open_kernel(mark_ref):
    mark_ref[...] = jnp.zeros_like(mark_ref)


def edge_kernel(mark_ref, count_ref, res_ref, cells_ref, outbox_ref, corner_ref, face_cell_ref,
                corner_cell_ref, msg0_ref, msg1_ref, ahead_ref, total_ref, wide_ref, terms_ref, stage_ref):
    total_ref[...] = jnp.zeros_like(total_ref)

    def count(k, width):
        return jnp.broadcast_to(count_ref[0:1, k : k + 1], (4, width))

    def living_of(width, offset):
        slot = lax.broadcasted_iota(jnp.int32, (4, width), 1)
        row = lax.broadcasted_iota(jnp.int32, (4, width), 0)
        counts = jnp.where(
            row < 2,
            jnp.where(row == 0, count(offset, width), count(offset + 1, width)),
            jnp.where(row == 2, count(offset + 2, width), count(offset + 3, width)),
        )
        return slot < counts

    face_cells = jnp.where(living_of(MIG, 0), face_cell_ref[...], -1).astype(F32)
    corner_cells = jnp.where(living_of(CORNER, 4), corner_cell_ref[...], -1).astype(F32)

    faces = [outbox_ref[c] for c in range(16)]
    corners = [corner_ref[c] for c in range(16)]

    for c, (face, corner) in enumerate(zip(faces + [face_cells], corners + [corner_cells])):
        for side in range(2):
            pair = join_pairs(corner, side, side + 2)
            if c < 16:
                stage_ref[side, 48 + c : 49 + c, :] = face[2 + side : 3 + side, 0:128]
                stage_ref[side, 64 + c : 65 + c, :] = face[2 + side : 3 + side, 128:256]
                stage_ref[side, 80 + c : 81 + c, :] = pair
                ahead_ref[side, c : c + 1, :] = face[side : side + 1, 0:128]
                ahead_ref[side, 16 + c : 17 + c, :] = face[side : side + 1, 128:256]
            else:
                stage_ref[side, 96:97, :] = face[2 + side : 3 + side, 0:128]
                stage_ref[side, 97:98, :] = face[2 + side : 3 + side, 128:256]
                stage_ref[side, 98:99, :] = pair
                stage_ref[side, 99:104, :] = jnp.zeros((5, 128), F32)
                ahead_ref[side, 32:33, :] = face[side : side + 1, 0:128]
                ahead_ref[side, 33:34, :] = face[side : side + 1, 128:256]
                ahead_ref[side, 34:40, :] = jnp.zeros((6, 128), F32)

    def wide(face, corner):
        pairs = jnp.concatenate([join_pairs(corner, 0, 1), join_pairs(corner, 2, 3)], axis=0)
        return jnp.concatenate([face[0:2, :], pairs], axis=1)

    state = [wide(faces[c], corners[c]) for c in range(16)] + [wide(face_cells, corner_cells)]
    for c, value in enumerate(state):
        wide_ref[c] = value
    deposit_wide(
        state[:16], state[16], total_ref, [0, 1, 2, 17, 18, 19, 100, 101], [(0, 3), (3, 3)]
    )

    state = [face[2:4, :] for face in faces]
    living, cell_x, _, cell_z = decode(face_cells[2:4, :])
    mass, carried, affine = deposit_terms(state, living)
    weights = [spline(state[axis]) for axis in range(3)]
    for g in range(2):
        depth = placed(NZ, MIG, row_of(cell_z, g), [row_of(w, g) for w in weights[2]])
        across, across_moment = placed(8, MIG, row_of(cell_x, g), [row_of(w, g) for w in weights[0]], 8)
        lines = []
        zero = jnp.zeros((8, MIG), F32)
        for c in range(4):
            for e in STEPS:
                weight = row_of(weights[1][e + 1], g)
                if c == 0:
                    plain, moment = (weight * row_of(mass, g)) * across, zero
                else:
                    base = row_of(carried[c - 1], g) + e * row_of(affine[3 * (c - 1) + 1], g)
                    plain = (weight * base) * across + (
                        weight * row_of(affine[3 * (c - 1)], g)
                    ) * across_moment
                    moment = (weight * row_of(affine[3 * (c - 1) + 2], g)) * across
                lines.append(jnp.concatenate([plain, moment], axis=1))
        product = scatter_product(jnp.concatenate(lines, axis=0), *depth)
        for c in range(4):
            for e in STEPS:
                at = ((CY if g == 0 else -1) + e + 2) * 8
                line = (3 * c + e + 1) * 8
                total_ref[c, at : at + 8, :] += product[line : line + 8, :]

    deposit_residents(res_ref, cells_ref, terms_ref, total_ref, 0, 2)
    deposit_residents(res_ref, cells_ref, terms_ref, total_ref, CY - 2, CY)

    for side in range(2):
        for pair in range(2):
            for j in range(3):
                at = ((CY + 1 + j) if side == 0 else j) * 8
                stage_ref[side, (3 * pair + j) * 8 : (3 * pair + j + 1) * 8, :] = fold_pair(
                    total_ref[2 * pair, at : at + 8, :], total_ref[2 * pair + 1, at : at + 8, :]
                )
    parity = lax.axis_index("gy") % 2
    msg0_ref[...] = stage_ref[parity]
    msg1_ref[...] = stage_ref[1 - parity]


def inner_kernel(res_ref, cells_ref, before_ref, wide_ref, grid_ref, total_ref, terms_ref):
    total_ref[...] = before_ref[...]
    deposit_wide(
        [wide_ref[c] for c in range(16)], wide_ref[16], total_ref, list(range(3, 19)), [(0, 14)]
    )
    deposit_residents(res_ref, cells_ref, terms_ref, total_ref, 2, CY - 2)
    for pair in range(2):
        for yy in range(YY):
            at = yy * 8
            grid_ref[pair, at : at + 8, :] = fold_pair(
                total_ref[2 * pair, at : at + 8, :], total_ref[2 * pair + 1, at : at + 8, :]
            )


def turn_kernel(grid_ref, in1_ref, in0_ref, ahead_ref, joined_ref, msg0_ref, msg1_ref, got_ref, stage_ref):
    parity = lax.axis_index("gy") % 2
    got_ref[parity] = in1_ref[...]
    got_ref[1 - parity] = in0_ref[...]
    joined_ref[...] = grid_ref[...]
    for pair in range(2):
        for j in range(3):
            line = (3 * pair + j) * 8
            for side, yy in ((0, 1 + j), (1, CY + j)):
                joined_ref[pair, yy * 8 : yy * 8 + 8, :] += got_ref[side, line : line + 8, :]
    low = low_half((16, 128))
    for side in range(2):
        for pair in range(2):
            for j in range(3):
                row = (3 + j) if side == 0 else (6 + j) % 8
                at = (3 * pair + j) * 18
                stage_ref[side, at : at + 18, :] = joined_ref[pair, pl.ds(8 + row, 18, stride=8), :]
        stage_ref[side, 108:112, :] = jnp.zeros((4, 128), F32)
        stage_ref[side, X_STATES : X_STATES + 32, :] = ahead_ref[side, 0:32, :]
        from_below, from_above = got_ref[0, 80:96, :], got_ref[1, 80:96, :]
        cell_below, cell_above = got_ref[0, 96:104, :], got_ref[1, 96:104, :]
        if side == 0:
            states = jnp.where(low, from_below, swap_half(from_above))
            cells = jnp.where(low[0:8], cell_below, swap_half(cell_above))
        else:
            states = jnp.where(low, swap_half(from_below), from_above)
            cells = jnp.where(low[0:8], swap_half(cell_below), cell_above)
        stage_ref[side, X_STATES + 32 : X_STATES + 48, :] = states
        stage_ref[side, X_STATES + 48 : X_STATES + 56, :] = jnp.zeros((8, 128), F32)
        stage_ref[side, X_STATES + 48 : X_STATES + 50, :] = ahead_ref[side, 32:34, :]
        stage_ref[side, X_STATES + 50 : X_STATES + 51, :] = cells[2:3, :]
    parity = lax.axis_index("gx") % 2
    msg0_ref[...] = stage_ref[parity]
    msg1_ref[...] = stage_ref[1 - parity]


def gather_product(nodes, depth_plain, depth_moment):
    low = low_half(nodes.shape)
    coarse = nodes.astype(BF16).astype(F32)
    lhs = jnp.where(low, coarse, nodes - coarse).astype(BF16)
    rhs = jnp.concatenate([depth_plain, depth_moment], axis=1)
    coarse, fine = split(rhs)
    dims = (((1,), (0,)), ((), ()))
    return lax.dot_general(
        lhs, jnp.concatenate([coarse, coarse], axis=0), dims, preferred_element_type=F32
    ) + lax.dot_general(lhs, jnp.concatenate([fine, fine], axis=0), dims, preferred_element_type=F32)


def contract(product, rows, width, normal, across, across_moment, normal_axis, across_axis):
    velocity, slopes = [], []
    for i in range(3):
        plain = [product[(3 * i + k) * rows : (3 * i + k + 1) * rows, 0:width] for k in range(3)]
        lifted = [
            product[(3 * i + k) * rows : (3 * i + k + 1) * rows, width : 2 * width] for k in range(3)
        ]
        low, mid, high = [normal[k] * plain[k] for k in range(3)]
        summed = low + mid + high
        stepped = high - low
        raised = normal[0] * lifted[0] + normal[1] * lifted[1] + normal[2] * lifted[2]
        velocity.append(jnp.sum(across * summed, axis=0, keepdims=True))
        slope = [None, None, jnp.sum(across * raised, axis=0, keepdims=True)]
        slope[normal_axis] = jnp.sum(across * stepped, axis=0, keepdims=True)
        slope[across_axis] = jnp.sum(across_moment * summed, axis=0, keepdims=True)
        slopes.append(slope)
    return velocity, slopes


def finished(state, living, velocity, slopes):
    out = [living * (state[k] + time_step * velocity[k]) for k in range(3)]
    out += [living * velocity[k] for k in range(3)]
    for i in range(3):
        out += [living * (4.0 * (slopes[i][k] - state[k] * velocity[i])) for k in range(3)]
    return out + [living * state[15]]


def last_kernel(res_ref, cells_ref, joined_ref, y1_ref, y0_ref, x1_ref, x0_ref,
                out_hbm, face_out_hbm, corner_out_hbm, got_y_ref, got_x_ref, grid_ref, vel_ref, near_ref,
                out_ref, face_out_ref, corner_out_ref, sems):
    parity = lax.axis_index("gy") % 2
    got_y_ref[parity] = y1_ref[...]
    got_y_ref[1 - parity] = y0_ref[...]
    parity = lax.axis_index("gx") % 2
    got_x_ref[parity] = x1_ref[...]
    got_x_ref[1 - parity] = x0_ref[...]

    grid_ref[...] = joined_ref[...]
    for side in range(2):
        for pair in range(2):
            for j in range(3):
                row = ((3 + j) if side == 0 else (6 + j) % 8) ^ 4
                at = (3 * pair + j) * 18
                grid_ref[pair, pl.ds(8 + row, 18, stride=8), :] += got_x_ref[side, at : at + 18, :]

    vel_ref[...] = jnp.zeros_like(vel_ref)
    low = low_half((8, 128))
    row = lax.broadcasted_iota(jnp.int32, (8, 128), 0)
    layer = lax.broadcasted_iota(jnp.int32, (8, 128), 1) % NZ
    inside = (layer > 0) & (layer < NZ - 1)
    upper = row < CX
    for yy in range(1, CY + 3):
        first = grid_ref[0, yy * 8 : yy * 8 + 8, :]
        second = grid_ref[1, yy * 8 : yy * 8 + 8, :]
        first_swap, second_swap = swap_half(first), swap_half(second)
        mass = jnp.maximum(jnp.where(low, first, first_swap), mass_floor)
        momentum = (
            jnp.where(low, first_swap, first),
            jnp.where(low, second, second_swap),
            jnp.where(low, second_swap, second),
        )
        for i in range(3):
            value = momentum[i] / mass
            if i == 2:
                value = value - time_step * gravity
            value = jnp.where(inside, value, 0.0)
            vel_ref[i, yy * 8 : yy * 8 + 8, :] = value
            for ex in STEPS:
                near = jnp.where(
                    upper,
                    pltpu.roll(value, (-ex) % 8, 0) if ex != 0 else value,
                    pltpu.roll(value, (CX - ex) % 8, 0),
                )
                near_ref[ex + 1, 1, i, yy - 1] = near
                near_ref[ex + 1, 0, i, yy - 1] = pltpu.roll(near, 1, 1)
                near_ref[ex + 1, 2, i, yy - 1] = pltpu.roll(near, 127, 1)

    copies = []
    for y in range(CY):
        state = [res_ref[c, y] for c in range(16)]
        living = resident_living(cells_ref, y)
        weights = [spline(state[axis]) for axis in range(3)]
        velocity, slopes = [], []
        for i in range(3):
            by_x = []
            for kx in range(3):
                by_y = []
                for ky in range(3):
                    low_z, mid_z, high_z = [
                        weights[2][kz] * near_ref[kx, kz, i, y + ky] for kz in range(3)
                    ]
                    by_y.append((low_z + mid_z + high_z, high_z - low_z))
                low_y, mid_y, high_y = [weights[1][k] * by_y[k][0] for k in range(3)]
                raised = (
                    weights[1][0] * by_y[0][1] + weights[1][1] * by_y[1][1] + weights[1][2] * by_y[2][1]
                )
                by_x.append((low_y + mid_y + high_y, high_y - low_y, raised))
            low_x, mid_x, high_x = [weights[0][k] * by_x[k][0] for k in range(3)]
            velocity.append(low_x + mid_x + high_x)
            slope = [high_x - low_x]
            for part in (1, 2):
                slope.append(
                    weights[0][0] * by_x[0][part]
                    + weights[0][1] * by_x[1][part]
                    + weights[0][2] * by_x[2][part]
                )
            slopes.append(slope)
        for c, value in enumerate(finished(state, living, velocity, slopes)):
            out_ref[c, y] = value
        if y % 4 == 3:
            copies.append(
                pltpu.make_async_copy(
                    out_ref.at[:, y - 3 : y + 1], out_hbm.at[:, y - 3 : y + 1], sems.at[y // 4]
                )
            )
            copies[-1].start()

    for side in range(2):
        def wide_row(k):
            return jnp.concatenate([got_x_ref[side, a : a + 1, :] for a in k], axis=1)

        base = X_STATES
        state = [wide_row((base + c, base + 16 + c, base + 32 + c)) for c in range(16)]
        number = wide_row((base + 48, base + 49, base + 50)).astype(jnp.int32)
        living = (number >= 0).astype(F32)
        weights = [spline(state[axis]) for axis in range(3)]
        depth = placed(NZ, WIDE, number % NZ, weights[2])
        across, across_moment = placed(YP, WIDE, (number // NZ) % CY + 2, weights[1])
        lines = []
        for i in range(3):
            for e in STEPS:
                at = ((0 if side == 0 else CX - 1) + e) % 8
                lines.append(vel_ref[i, pl.ds(at, YP, stride=8), :])
        product = gather_product(jnp.concatenate(lines, axis=0), *depth)
        velocity, slopes = contract(product, YP, WIDE, weights[0], across, across_moment, 0, 1)
        for c, value in enumerate(finished(state, living, velocity, slopes)):
            face_out_ref[c, side : side + 1, :] = value[:, 0:MIG]
            corner_out_ref[c, 2 * side : 2 * side + 1, :] = value[:, MIG : MIG + CORNER]
            corner_out_ref[c, 2 * side + 1 : 2 * side + 2, :] = value[:, MIG + CORNER : WIDE]

    for side in range(2):
        def face_row(k):
            return jnp.concatenate([got_y_ref[side, a : a + 1, :] for a in k], axis=1)

        state = [face_row((48 + c, 64 + c)) for c in range(16)]
        number = face_row((96, 97)).astype(jnp.int32)
        living = (number >= 0).astype(F32)
        weights = [spline(state[axis]) for axis in range(3)]
        depth = placed(NZ, MIG, number % NZ, weights[2])
        across, across_moment = placed(8, MIG, jnp.maximum(number, 0) // (CY * NZ), weights[0], 8)
        lines = []
        for i in range(3):
            for e in STEPS:
                at = ((0 if side == 0 else CY - 1) + 2 + e) * 8
                lines.append(vel_ref[i, at : at + 8, :])
        product = gather_product(jnp.concatenate(lines, axis=0), *depth)
        velocity, slopes = contract(product, 8, MIG, weights[1], across, across_moment, 1, 0)
        for c, value in enumerate(finished(state, living, velocity, slopes)):
            face_out_ref[c, 2 + side : 3 + side, :] = value

    copies.append(pltpu.make_async_copy(face_out_ref, face_out_hbm, sems.at[4]))
    copies.append(pltpu.make_async_copy(corner_out_ref, corner_out_hbm, sems.at[5]))
    for copy in copies[-2:]:
        copy.start()
    for copy in copies:
        copy.wait()


def partner(index, phase, count):
    return (((index - phase) % count ^ 1) + phase) % count


def swapped(value, axis, phase):
    count = lax.axis_size(axis)
    return lax.ppermute(value, axis, [(i, partner(i, phase, count)) for i in range(count)])


VMEM = pl.BlockSpec(memory_space=pltpu.VMEM)
HBM = pl.BlockSpec(memory_space=pltpu.HBM)


def scratch(shape, dtype=F32):
    return pltpu.VMEM(shape, dtype)


def call(kernel, in_specs, out_spec, out_shapes, scratch_shapes, flops):
    return pl.pallas_call(
        kernel,
        in_specs=in_specs,
        out_specs=[out_spec] * len(out_shapes),
        out_shape=[jax.ShapeDtypeStruct(shape, F32) for shape in out_shapes],
        scratch_shapes=scratch_shapes,
        compiler_params=pltpu.CompilerParams(vmem_limit_bytes=24 * 1024 * 1024),
        cost_estimate=pl.CostEstimate(flops=flops, bytes_accessed=1 << 20, transcendentals=0),
    )


def body(residents, cell_count, outbox, corner_box, face_cell, corner_cell, mig_count):
    res = residents.reshape(16, CX, CY, 2, 128).transpose(0, 2, 3, 1, 4).reshape(16, CY, 8, 128)
    (mark,) = call(open_kernel, [], VMEM, [(8, 128)], [], 10_000_000_000)()
    msg0, msg1, ahead, total, wide = call(
        edge_kernel,
        [VMEM] * 8,
        VMEM,
        [(Y_ROWS, 128), (Y_ROWS, 128), (2, 40, 128), (4, YP * 8, 128), (17, 2, WIDE)],
        [scratch((CY, 22, 8, 128)), scratch((2, Y_ROWS, 128))],
        10_000_000,
    )(mark, mig_count.reshape(1, 8), res, cell_count, outbox, corner_box, face_cell, corner_cell)
    y0 = swapped(msg0, "gy", 0)
    y1 = swapped(msg1, "gy", 1)
    (grid,) = call(
        inner_kernel,
        [VMEM] * 4,
        VMEM,
        [(2, YY * 8, 128)],
        [scratch((4, YP * 8, 128)), scratch((CY, 22, 8, 128))],
        10_000_000,
    )(res, cell_count, total, wide)
    joined, msg0, msg1 = call(
        turn_kernel,
        [VMEM] * 4,
        VMEM,
        [(2, YY * 8, 128), (X_ROWS, 128), (X_ROWS, 128)],
        [scratch((2, Y_ROWS, 128)), scratch((2, X_ROWS, 128))],
        1_000_000,
    )(grid, y1, y0, ahead)
    x0 = swapped(msg0, "gx", 0)
    x1 = swapped(msg1, "gx", 1)
    out, face_out, corner_out = call(
        last_kernel,
        [VMEM] * 7,
        HBM,
        [(16, CY, 8, 128), (16, 4, MIG), (16, 4, CORNER)],
        [
            scratch((2, Y_ROWS, 128)),
            scratch((2, X_ROWS, 128)),
            scratch((2, YY * 8, 128)),
            scratch((3, YP * 8, 128)),
            scratch((3, 3, 3, CY + 2, 8, 128)),
            scratch((16, CY, 8, 128)),
            scratch((16, 4, MIG)),
            scratch((16, 4, CORNER)),
            pltpu.SemaphoreType.DMA((6,)),
        ],
        10_000_000,
    )(res, cell_count, joined, y1, y0, x1, x0)
    out = out.reshape(16, CY, 2, CX, 128).transpose(0, 3, 1, 2, 4).reshape(16, CX, CY * 256)
    return out, face_out, corner_out


def solution(mesh):
    in_specs = (
        P(None, "gx", "gy"),
        P("gx", "gy"),
        P(None, "gx", "gy"),
        P(None, "gx", "gy"),
        P("gx", "gy"),
        P("gx", "gy"),
        P("gx", "gy"),
    )
    out_specs = (P(None, "gx", "gy"), P(None, "gx", "gy"), P(None, "gx", "gy"))
    return jax.shard_map(body, mesh=mesh, in_specs=in_specs, out_specs=out_specs, check_vma=False)
```

```python
import jax
import jax.numpy as jnp
from jax import lax
from jax.experimental import pallas as pl
from jax.experimental.pallas import tpu as pltpu
from jax.sharding import PartitionSpec as P

CX = 4
CY = 16
NZ = 64
MIG = 256
CORNER = 64
PAIR = 2 * CORNER
WIDE = MIG + PAIR
YY = 20
YP = 24
Y_ROWS = 104
Y_STATES = 48
X_ROWS = 160
X_STATES = 112
time_step = 0.1
gravity = 1.0
mass_floor = 0.5
STEPS = (-1, 0, 1)
F32 = jnp.float32
BF16 = jnp.bfloat16


def spline(offset):
    low = 0.5 - offset
    high = 0.5 + offset
    return (0.5 * (low * low), 0.75 - offset * offset, 0.5 * (high * high))


def deposit_terms(state, living):
    mass = state[15] * living
    affine = [mass * state[6 + j] for j in range(9)]
    carried = []
    for i in range(3):
        skew = affine[3 * i] * state[0] + affine[3 * i + 1] * state[1] + affine[3 * i + 2] * state[2]
        carried.append(mass * state[3 + i] - skew)
    return mass, carried, affine


def placed(rows, width, cell, weights, row=None):
    if row is None:
        row = lax.broadcasted_iota(jnp.int32, (rows, width), 0)
    step = row - cell
    low, mid, high = weights
    zero = jnp.zeros((rows, width), F32)
    is_low, is_high = step == -1, step == 1
    moment = jnp.where(is_low, -low, jnp.where(is_high, high, zero))
    plain = jnp.where(is_low, low, jnp.where(is_high, high, jnp.where(step == 0, mid, zero)))
    return plain, moment


def split(value):
    coarse = value.astype(BF16)
    fine = (value - coarse.astype(F32)).astype(BF16)
    return coarse, fine


def low_half(shape):
    return lax.broadcasted_iota(jnp.int32, shape, len(shape) - 1) % 128 < NZ


def swap_half(value):
    return pltpu.roll(value, NZ, value.ndim - 1)


def scatter_product(lhs, depth_plain, depth_moment):
    rhs = jnp.concatenate([depth_plain, depth_moment], axis=1)
    rhs = jnp.concatenate(split(rhs), axis=0)
    rows = lhs.shape[0]
    product = lax.dot_general(
        jnp.concatenate(split(lhs), axis=0), rhs, (((1,), (1,)), ((), ())), preferred_element_type=F32
    )
    return product[0:rows] + product[rows : 2 * rows]


def row_of(value, g):
    return value[g : g + 1, :]


def join_pairs(value, first, second):
    return jnp.concatenate([value[first : first + 1, :], value[second : second + 1, :]], axis=1)


def fold_pair(first, second):
    low = low_half(first.shape)
    return jnp.where(low, first, second) + swap_half(jnp.where(low, second, first))


def resident_living(count_ref, y):
    lane = 128 * (y // 2)
    counts = count_ref[:, lane : lane + 128]
    low = low_half(counts.shape)
    if y % 2 == 0:
        counts = jnp.where(low, counts, swap_half(counts))
    else:
        counts = jnp.where(low, swap_half(counts), counts)
    counts = jnp.concatenate([counts, counts], axis=0)
    row = lax.broadcasted_iota(jnp.int32, (8, 128), 0)
    lane_id = lax.broadcasted_iota(jnp.int32, (8, 128), 1)
    slot = 2 * (row // CX) + lane_id // NZ
    return (slot < counts).astype(F32)


def deposit_residents(res_ref, count_ref, terms_ref, shift_ref, total_ref, first, last):
    row = lax.broadcasted_iota(jnp.int32, (8, 128), 0)
    for y in range(first, last):
        state = [res_ref[c, y] for c in range(16)]
        mass, carried, affine = deposit_terms(state, resident_living(count_ref, y))
        stored = [mass] + carried + affine
        for axis in range(3):
            stored += list(spline(state[axis]))
        for k, value in enumerate(stored):
            terms_ref[y, k] = value
    for ex in STEPS:
        sums = {}

        def finish_node(node):
            for c in range(4):
                value = (
                    sums.pop((node, c, 0))
                    + pltpu.roll(sums.pop((node, c, 1)), 1, 1)
                    + pltpu.roll(sums.pop((node, c, -1)), 127, 1)
                )
                at = (node + 2) * 8
                shift_ref[ex + 1, c, at : at + 8, :] = value

        for y in range(first, last):
            term = [terms_ref[y, k] for k in range(13)]
            weight_x = terms_ref[y, 13 + ex + 1]
            weight_y = [terms_ref[y, 16 + k] for k in range(3)]
            along = [term[0]]
            for i in range(3):
                value = term[1 + i]
                if ex != 0:
                    value = value + term[4 + 3 * i] if ex > 0 else value - term[4 + 3 * i]
                along.append(value)
            for ez in STEPS:
                weight = weight_x * terms_ref[y, 19 + ez + 1]
                for c in range(4):
                    value = along[c]
                    if c > 0 and ez != 0:
                        lift = term[4 + 3 * (c - 1) + 2]
                        value = value + lift if ez > 0 else value - lift
                    value = weight * value
                    parts = [value, value, value]
                    if c > 0:
                        lean = weight * term[4 + 3 * (c - 1) + 1]
                        parts = [value - lean, value, value + lean]
                    for ey in STEPS:
                        key = (y + ey, c, ez)
                        part = weight_y[ey + 1] * parts[ey + 1]
                        sums[key] = sums[key] + part if key in sums else part
            finish_node(y - 1)
        finish_node(last - 1)
        finish_node(last)
    for node in range(first - 1, last + 1):
        at = (node + 2) * 8
        for c in range(4):
            value = total_ref[c, at : at + 8, :]
            for ex in STEPS:
                low = at - 2 - ex
                both = shift_ref[ex + 1, c, low : low + 8, :] + shift_ref[ex + 1, c, low + 4 : low + 12, :]
                value = value + jnp.where((row >= 2 + ex) & (row < 2 + ex + CX), both, 0.0)
            total_ref[c, at : at + 8, :] = value


def decode(cells):
    number = cells.astype(jnp.int32)
    living = (number >= 0).astype(F32)
    return living, number // (CY * NZ), (number // NZ) % CY, number % NZ


def deposit_wide(state, cells, total_ref, row_nodes, chunks):
    rows = len(row_nodes)
    living, _, cell_y, cell_z = decode(cells)
    lane = lax.broadcasted_iota(jnp.int32, (2, WIDE), 1)
    cell_y = cell_y + jnp.where(lane < MIG, 2, jnp.where(lane < MIG + CORNER, 2 + CY, 2 - CY))
    mass, carried, affine = deposit_terms(state, living)
    weights = [spline(state[axis]) for axis in range(3)]
    row = lax.broadcasted_iota(jnp.int32, (rows, WIDE), 0)
    node = row
    for k in range(rows):
        if k == 0:
            node = row + row_nodes[0]
        elif row_nodes[k] != row_nodes[k - 1] + 1:
            node = jnp.where(row >= k, row + (row_nodes[k] - k), node)
    for g in range(2):
        depth = placed(NZ, WIDE, row_of(cell_z, g), [row_of(w, g) for w in weights[2]])
        across, across_moment = placed(
            rows, WIDE, row_of(cell_y, g), [row_of(w, g) for w in weights[1]], row=node
        )
        lines = []
        zero = jnp.zeros((rows, WIDE), F32)
        for c in range(4):
            for e in STEPS:
                weight = row_of(weights[0][e + 1], g)
                if c == 0:
                    plain, moment = (weight * row_of(mass, g)) * across, zero
                else:
                    base = row_of(carried[c - 1], g) + e * row_of(affine[3 * (c - 1)], g)
                    plain = (weight * base) * across + (
                        weight * row_of(affine[3 * (c - 1) + 1], g)
                    ) * across_moment
                    moment = (weight * row_of(affine[3 * (c - 1) + 2], g)) * across
                lines.append(jnp.concatenate([plain, moment], axis=1))
        product = scatter_product(jnp.concatenate(lines, axis=0), *depth)
        for c in range(4):
            for e in STEPS:
                row = (CX if g == 0 else -1) + e + 2
                for start, count in chunks:
                    at = (3 * c + e + 1) * rows + start
                    total_ref[c, pl.ds(row_nodes[start] * 8 + row, count, stride=8), :] += product[
                        at : at + count, :
                    ]


def open_kernel(mark_ref):
    mark_ref[...] = jnp.zeros_like(mark_ref)


def leave_kernel(mark_ref, count_ref, outbox_ref, corner_ref, face_cell_ref, corner_cell_ref,
                 total_ref, stage_ref, ahead_ref, wide_ref):
    total_ref[...] = jnp.zeros_like(total_ref)

    def count(k, width):
        return jnp.broadcast_to(count_ref[0:1, k : k + 1], (4, width))

    def living_of(width, offset):
        slot = lax.broadcasted_iota(jnp.int32, (4, width), 1)
        row = lax.broadcasted_iota(jnp.int32, (4, width), 0)
        counts = jnp.where(
            row < 2,
            jnp.where(row == 0, count(offset, width), count(offset + 1, width)),
            jnp.where(row == 2, count(offset + 2, width), count(offset + 3, width)),
        )
        return slot < counts

    face_cells = jnp.where(living_of(MIG, 0), face_cell_ref[...], -1).astype(F32)
    corner_cells = jnp.where(living_of(CORNER, 4), corner_cell_ref[...], -1).astype(F32)

    faces = [outbox_ref[c] for c in range(16)]
    corners = [corner_ref[c] for c in range(16)]

    for c, (face, corner) in enumerate(zip(faces + [face_cells], corners + [corner_cells])):
        for side in range(2):
            pair = join_pairs(corner, side, side + 2)
            if c < 16:
                stage_ref[side, c : 1 + c, :] = face[2 + side : 3 + side, 0:128]
                stage_ref[side, 16 + c : 17 + c, :] = face[2 + side : 3 + side, 128:256]
                stage_ref[side, 32 + c : 33 + c, :] = pair
                ahead_ref[side, c : c + 1, :] = face[side : side + 1, 0:128]
                ahead_ref[side, 16 + c : 17 + c, :] = face[side : side + 1, 128:256]
            else:
                stage_ref[side, 48:49, :] = face[2 + side : 3 + side, 0:128]
                stage_ref[side, 49:50, :] = face[2 + side : 3 + side, 128:256]
                stage_ref[side, 50:51, :] = pair
                stage_ref[side, 51:56, :] = jnp.zeros((5, 128), F32)
                ahead_ref[side, 32:33, :] = face[side : side + 1, 0:128]
                ahead_ref[side, 33:34, :] = face[side : side + 1, 128:256]
                ahead_ref[side, 34:40, :] = jnp.zeros((6, 128), F32)

    def wide(face, corner):
        pairs = jnp.concatenate([join_pairs(corner, 0, 1), join_pairs(corner, 2, 3)], axis=0)
        return jnp.concatenate([face[0:2, :], pairs], axis=1)

    state = [wide(faces[c], corners[c]) for c in range(16)] + [wide(face_cells, corner_cells)]
    for c, value in enumerate(state):
        wide_ref[c] = value
    deposit_wide(
        state[:16], state[16], total_ref, [0, 1, 2, 17, 18, 19, 100, 101], [(0, 3), (3, 3)]
    )

    state = [face[2:4, :] for face in faces]
    living, cell_x, _, cell_z = decode(face_cells[2:4, :])
    mass, carried, affine = deposit_terms(state, living)
    weights = [spline(state[axis]) for axis in range(3)]
    for g in range(2):
        depth = placed(NZ, MIG, row_of(cell_z, g), [row_of(w, g) for w in weights[2]])
        across, across_moment = placed(8, MIG, row_of(cell_x, g) + 2, [row_of(w, g) for w in weights[0]])
        lines = []
        zero = jnp.zeros((8, MIG), F32)
        for c in range(4):
            for e in STEPS:
                weight = row_of(weights[1][e + 1], g)
                if c == 0:
                    plain, moment = (weight * row_of(mass, g)) * across, zero
                else:
                    base = row_of(carried[c - 1], g) + e * row_of(affine[3 * (c - 1) + 1], g)
                    plain = (weight * base) * across + (
                        weight * row_of(affine[3 * (c - 1)], g)
                    ) * across_moment
                    moment = (weight * row_of(affine[3 * (c - 1) + 2], g)) * across
                lines.append(jnp.concatenate([plain, moment], axis=1))
        product = scatter_product(jnp.concatenate(lines, axis=0), *depth)
        for c in range(4):
            for e in STEPS:
                at = ((CY if g == 0 else -1) + e + 2) * 8
                line = (3 * c + e + 1) * 8
                total_ref[c, at : at + 8, :] += product[line : line + 8, :]


def edge_kernel(res_ref, cells_ref, states_ref, before_ref, msg0_ref, msg1_ref, total_ref,
                terms_ref, shift_ref, stage_ref):
    total_ref[...] = before_ref[...]
    deposit_residents(res_ref, cells_ref, terms_ref, shift_ref, total_ref, 0, 2)
    deposit_residents(res_ref, cells_ref, terms_ref, shift_ref, total_ref, CY - 2, CY)

    for side in range(2):
        for pair in range(2):
            for j in range(3):
                at = ((CY + 1 + j) if side == 0 else j) * 8
                stage_ref[side, (3 * pair + j) * 8 : (3 * pair + j + 1) * 8, :] = fold_pair(
                    total_ref[2 * pair, at : at + 8, :], total_ref[2 * pair + 1, at : at + 8, :]
                )
    parity = lax.axis_index("gy") % 2
    for msg_ref, side in ((msg0_ref, parity), (msg1_ref, 1 - parity)):
        msg_ref[0:Y_STATES, :] = stage_ref[side]
        msg_ref[Y_STATES:Y_ROWS, :] = states_ref[side]


def inner_kernel(res_ref, cells_ref, before_ref, wide_ref, grid_ref, total_ref, terms_ref, shift_ref):
    total_ref[...] = before_ref[...]
    deposit_wide(
        [wide_ref[c] for c in range(16)], wide_ref[16], total_ref, list(range(3, 19)), [(0, 14)]
    )
    deposit_residents(res_ref, cells_ref, terms_ref, shift_ref, total_ref, 2, CY - 2)
    for pair in range(2):
        for yy in range(YY):
            at = yy * 8
            grid_ref[pair, at : at + 8, :] = fold_pair(
                total_ref[2 * pair, at : at + 8, :], total_ref[2 * pair + 1, at : at + 8, :]
            )


def turn_kernel(grid_ref, in1_ref, in0_ref, ahead_ref, joined_ref, msg0_ref, msg1_ref, got_ref, stage_ref):
    parity = lax.axis_index("gy") % 2
    got_ref[parity] = in1_ref[...]
    got_ref[1 - parity] = in0_ref[...]
    joined_ref[...] = grid_ref[...]
    for pair in range(2):
        for j in range(3):
            line = (3 * pair + j) * 8
            for side, yy in ((0, 1 + j), (1, CY + j)):
                joined_ref[pair, yy * 8 : yy * 8 + 8, :] += got_ref[side, line : line + 8, :]
    low = low_half((16, 128))
    for side in range(2):
        for pair in range(2):
            for j in range(3):
                row = (5 + j) if side == 0 else j
                at = (3 * pair + j) * 18
                stage_ref[side, at : at + 18, :] = joined_ref[pair, pl.ds(8 + row, 18, stride=8), :]
        stage_ref[side, X_STATES : X_STATES + 32, :] = ahead_ref[side, 0:32, :]
        from_below, from_above = got_ref[0, 80:96, :], got_ref[1, 80:96, :]
        cell_below, cell_above = got_ref[0, 96:104, :], got_ref[1, 96:104, :]
        if side == 0:
            states = jnp.where(low, from_below, swap_half(from_above))
            cells = jnp.where(low[0:8], cell_below, swap_half(cell_above))
        else:
            states = jnp.where(low, swap_half(from_below), from_above)
            cells = jnp.where(low[0:8], swap_half(cell_below), cell_above)
        stage_ref[side, X_STATES + 32 : X_STATES + 48, :] = states
        stage_ref[side, 108:110, :] = ahead_ref[side, 32:34, :]
        stage_ref[side, 110:111, :] = cells[2:3, :]
        stage_ref[side, 111:112, :] = jnp.zeros((1, 128), F32)
    parity = lax.axis_index("gx") % 2
    msg0_ref[...] = stage_ref[parity]
    msg1_ref[...] = stage_ref[1 - parity]


def gather_product(nodes, depth_plain, depth_moment):
    low = low_half(nodes.shape)
    coarse = nodes.astype(BF16).astype(F32)
    lhs = jnp.where(low, coarse, nodes - coarse).astype(BF16)
    rhs = jnp.concatenate([depth_plain, depth_moment], axis=1)
    coarse, fine = split(rhs)
    dims = (((1,), (0,)), ((), ()))
    return lax.dot_general(
        lhs, jnp.concatenate([coarse, coarse], axis=0), dims, preferred_element_type=F32
    ) + lax.dot_general(lhs, jnp.concatenate([fine, fine], axis=0), dims, preferred_element_type=F32)


def contract(product, rows, width, normal, across, across_moment, normal_axis, across_axis):
    velocity, slopes = [], []
    for i in range(3):
        plain = [product[(3 * i + k) * rows : (3 * i + k + 1) * rows, 0:width] for k in range(3)]
        lifted = [
            product[(3 * i + k) * rows : (3 * i + k + 1) * rows, width : 2 * width] for k in range(3)
        ]
        low, mid, high = [normal[k] * plain[k] for k in range(3)]
        summed = low + mid + high
        stepped = high - low
        raised = normal[0] * lifted[0] + normal[1] * lifted[1] + normal[2] * lifted[2]
        velocity.append(jnp.sum(across * summed, axis=0, keepdims=True))
        slope = [None, None, jnp.sum(across * raised, axis=0, keepdims=True)]
        slope[normal_axis] = jnp.sum(across * stepped, axis=0, keepdims=True)
        slope[across_axis] = jnp.sum(across_moment * summed, axis=0, keepdims=True)
        slopes.append(slope)
    return velocity, slopes


def finished(state, living, velocity, slopes):
    out = [living * state[k] + (0.25 * time_step) * velocity[k] for k in range(3)]
    out += [0.25 * velocity[k] for k in range(3)]
    for i in range(3):
        out += [slopes[i][k] - state[k] * velocity[i] for k in range(3)]
    return out + [living * state[15]]


def both(first, second):
    return jnp.concatenate([first, second], axis=0)


def last_kernel(res_ref, cells_ref, joined_ref, y1_ref, y0_ref, x1_ref, x0_ref,
                out_hbm, face_out_hbm, corner_out_hbm, got_y_ref, got_x_ref, grid_ref, vel_ref, near_ref,
                out_ref, face_out_ref, corner_out_ref, sems):
    parity = lax.axis_index("gy") % 2
    got_y_ref[parity] = y1_ref[...]
    got_y_ref[1 - parity] = y0_ref[...]
    parity = lax.axis_index("gx") % 2
    got_x_ref[parity] = x1_ref[...]
    got_x_ref[1 - parity] = x0_ref[...]

    grid_ref[...] = joined_ref[...]
    for side in range(2):
        for pair in range(2):
            for j in range(3):
                row = (1 + j) if side == 0 else (4 + j)
                at = (3 * pair + j) * 18
                grid_ref[pair, pl.ds(8 + row, 18, stride=8), :] += got_x_ref[side, at : at + 18, :]

    vel_ref[...] = jnp.zeros_like(vel_ref)
    low = low_half((8, 128))
    row = lax.broadcasted_iota(jnp.int32, (8, 128), 0)
    layer = lax.broadcasted_iota(jnp.int32, (8, 128), 1) % NZ
    inside = (layer > 0) & (layer < NZ - 1)
    upper = row < CX
    for yy in range(1, CY + 3):
        first = grid_ref[0, yy * 8 : yy * 8 + 8, :]
        second = grid_ref[1, yy * 8 : yy * 8 + 8, :]
        first_swap, second_swap = swap_half(first), swap_half(second)
        share = 1.0 / (0.25 * jnp.maximum(jnp.where(low, first, first_swap), mass_floor))
        momentum = (
            jnp.where(low, first_swap, first),
            jnp.where(low, second, second_swap),
            jnp.where(low, second_swap, second),
        )
        for i in range(3):
            value = (0.25 * momentum[i]) * share
            if i == 2:
                value = value - time_step * gravity
            vel_ref[i, yy * 8 : yy * 8 + 8, :] = jnp.where(inside, value, 0.0)
    for yy in range(1, CY + 3):
        for i in range(3):
            for ex in STEPS:
                at = yy * 8 + ex
                near = jnp.where(upper, vel_ref[i, at + 2 : at + 10, :], vel_ref[i, at - 2 : at + 6, :])
                near_ref[ex + 1, 1, i, yy - 1] = near
                near_ref[ex + 1, 0, i, yy - 1] = pltpu.roll(near, 1, 1)
                near_ref[ex + 1, 2, i, yy - 1] = pltpu.roll(near, 127, 1)

    copies = []
    for y in range(CY):
        state = [res_ref[c, y] for c in range(16)]
        living = resident_living(cells_ref, y)
        weights = [spline(state[axis]) for axis in range(3)]
        scale = 4.0 * living
        weights[0] = [scale * value for value in weights[0]]
        velocity, slopes = [], []
        for i in range(3):
            by_x = []
            for kx in range(3):
                by_y = []
                for ky in range(3):
                    low_z, mid_z, high_z = [
                        weights[2][kz] * near_ref[kx, kz, i, y + ky] for kz in range(3)
                    ]
                    by_y.append((low_z + mid_z + high_z, high_z - low_z))
                low_y, mid_y, high_y = [weights[1][k] * by_y[k][0] for k in range(3)]
                raised = (
                    weights[1][0] * by_y[0][1] + weights[1][1] * by_y[1][1] + weights[1][2] * by_y[2][1]
                )
                by_x.append((low_y + mid_y + high_y, high_y - low_y, raised))
            low_x, mid_x, high_x = [weights[0][k] * by_x[k][0] for k in range(3)]
            velocity.append(low_x + mid_x + high_x)
            slope = [high_x - low_x]
            for part in (1, 2):
                slope.append(
                    weights[0][0] * by_x[0][part]
                    + weights[0][1] * by_x[1][part]
                    + weights[0][2] * by_x[2][part]
                )
            slopes.append(slope)
        for c, value in enumerate(finished(state, living, velocity, slopes)):
            out_ref[c, y] = value
        if y % 4 == 3:
            copies.append(
                pltpu.make_async_copy(
                    out_ref.at[:, y - 3 : y + 1], out_hbm.at[:, y - 3 : y + 1], sems.at[y // 4]
                )
            )
            copies[-1].start()

    def rows_of(got_ref, lines):
        return jnp.concatenate(
            [both(got_ref[0, a : a + 1, :], got_ref[1, a : a + 1, :]) for a in lines], axis=1
        )

    def prepared(got_ref, lines, cell_lines):
        state = [rows_of(got_ref, [a + c for a in lines]) for c in range(16)]
        number = rows_of(got_ref, cell_lines).astype(jnp.int32)
        living = (number >= 0).astype(F32)
        weights = [spline(state[axis]) for axis in range(3)]
        return state, number, living, weights

    def gathered(side, nodes, rows, width, number, across_cell, weights, scale, normal_axis, across_axis):
        picked = [[row_of(value, side) for value in weights[axis]] for axis in range(3)]
        depth = placed(NZ, width, row_of(number % NZ, side), picked[2])
        across, across_moment = placed(rows, width, row_of(across_cell, side), picked[across_axis])
        product = gather_product(jnp.concatenate(nodes, axis=0), *depth)
        normal = [row_of(scale, side) * value for value in picked[normal_axis]]
        return contract(product, rows, width, normal, across, across_moment, normal_axis, across_axis)

    def joined_sides(parts):
        velocity = [both(parts[0][0][i], parts[1][0][i]) for i in range(3)]
        slopes = [[both(parts[0][1][i][k], parts[1][1][i][k]) for k in range(3)] for i in range(3)]
        return velocity, slopes

    state, number, living, weights = prepared(
        got_x_ref, (X_STATES, X_STATES + 16, X_STATES + 32), (108, 109, 110)
    )
    parts = []
    for side in range(2):
        first = (0 if side == 0 else CX - 1) + 2
        nodes = [vel_ref[i, pl.ds(first + e, YP, stride=8), :] for i in range(3) for e in STEPS]
        parts.append(
            gathered(side, nodes, YP, WIDE, number, (number // NZ) % CY + 2, weights, 4.0 * living, 0, 1)
        )
    for c, value in enumerate(finished(state, living, *joined_sides(parts))):
        face_out_ref[c, 0:2, :] = value[:, 0:MIG]
        for side in range(2):
            corner_out_ref[c, 2 * side : 2 * side + 1, :] = row_of(value, side)[:, MIG : MIG + CORNER]
            corner_out_ref[c, 2 * side + 1 : 2 * side + 2, :] = row_of(value, side)[:, MIG + CORNER : WIDE]

    state, number, living, weights = prepared(got_y_ref, (48, 64), (96, 97))
    parts = []
    for side in range(2):
        first = (0 if side == 0 else CY - 1) + 2
        nodes = [
            vel_ref[i, (first + e) * 8 : (first + e) * 8 + 8, :] for i in range(3) for e in STEPS
        ]
        parts.append(
            gathered(side, nodes, 8, MIG, number, number // (CY * NZ) + 2, weights, 4.0 * living, 1, 0)
        )
    for c, value in enumerate(finished(state, living, *joined_sides(parts))):
        face_out_ref[c, 2:4, :] = value

    copies.append(pltpu.make_async_copy(face_out_ref, face_out_hbm, sems.at[4]))
    copies.append(pltpu.make_async_copy(corner_out_ref, corner_out_hbm, sems.at[5]))
    for copy in copies[-2:]:
        copy.start()
    for copy in copies:
        copy.wait()


def partner(index, phase, count):
    return (((index - phase) % count ^ 1) + phase) % count


def swapped(value, axis, phase):
    count = lax.axis_size(axis)
    return lax.ppermute(value, axis, [(i, partner(i, phase, count)) for i in range(count)])


VMEM = pl.BlockSpec(memory_space=pltpu.VMEM)
HBM = pl.BlockSpec(memory_space=pltpu.HBM)


def scratch(shape, dtype=F32):
    return pltpu.VMEM(shape, dtype)


def call(kernel, in_specs, out_spec, out_shapes, scratch_shapes, flops):
    return pl.pallas_call(
        kernel,
        in_specs=in_specs,
        out_specs=[out_spec] * len(out_shapes),
        out_shape=[jax.ShapeDtypeStruct(shape, F32) for shape in out_shapes],
        scratch_shapes=scratch_shapes,
        compiler_params=pltpu.CompilerParams(vmem_limit_bytes=24 * 1024 * 1024),
        cost_estimate=pl.CostEstimate(flops=flops, bytes_accessed=1 << 20, transcendentals=0),
    )


def body(residents, cell_count, outbox, corner_box, face_cell, corner_cell, mig_count):
    res = residents.reshape(16, CX, CY, 2, 128).transpose(0, 2, 3, 1, 4).reshape(16, CY, 8, 128)
    (mark,) = call(open_kernel, [], VMEM, [(8, 128)], [], 10_000_000_000)()
    left, states, ahead, wide = call(
        leave_kernel,
        [VMEM] * 6,
        VMEM,
        [(4, YP * 8, 128), (2, Y_ROWS - Y_STATES, 128), (2, 40, 128), (17, 2, WIDE)],
        [],
        10_000_000,
    )(mark, mig_count.reshape(1, 8), outbox, corner_box, face_cell, corner_cell)
    msg0, msg1, total = call(
        edge_kernel,
        [VMEM] * 4,
        VMEM,
        [(Y_ROWS, 128), (Y_ROWS, 128), (4, YP * 8, 128)],
        [scratch((CY, 22, 8, 128)), scratch((3, 4, YP * 8, 128)), scratch((2, Y_STATES, 128))],
        10_000_000,
    )(res, cell_count, states, left)
    y0 = swapped(msg0, "gy", 0)
    y1 = swapped(msg1, "gy", 1)
    (grid,) = call(
        inner_kernel,
        [VMEM] * 4,
        VMEM,
        [(2, YY * 8, 128)],
        [scratch((4, YP * 8, 128)), scratch((CY, 22, 8, 128)), scratch((3, 4, YP * 8, 128))],
        10_000_000,
    )(res, cell_count, total, wide)
    joined, msg0, msg1 = call(
        turn_kernel,
        [VMEM] * 4,
        VMEM,
        [(2, YY * 8, 128), (X_ROWS, 128), (X_ROWS, 128)],
        [scratch((2, Y_ROWS, 128)), scratch((2, X_ROWS, 128))],
        1_000_000,
    )(grid, y1, y0, ahead)
    x0 = swapped(msg0, "gx", 0)
    x1 = swapped(msg1, "gx", 1)
    out, face_out, corner_out = call(
        last_kernel,
        [VMEM] * 7,
        HBM,
        [(16, CY, 8, 128), (16, 4, MIG), (16, 4, CORNER)],
        [
            scratch((2, Y_ROWS, 128)),
            scratch((2, X_ROWS, 128)),
            scratch((2, YY * 8, 128)),
            scratch((3, YP * 8, 128)),
            scratch((3, 3, 3, CY + 2, 8, 128)),
            scratch((16, CY, 8, 128)),
            scratch((16, 4, MIG)),
            scratch((16, 4, CORNER)),
            pltpu.SemaphoreType.DMA((6,)),
        ],
        10_000_000,
    )(res, cell_count, joined, y1, y0, x1, x0)
    out = out.reshape(16, CY, 2, CX, 128).transpose(0, 3, 1, 2, 4).reshape(16, CX, CY * 256)
    return out, face_out, corner_out


def solution(mesh):
    in_specs = (
        P(None, "gx", "gy"),
        P("gx", "gy"),
        P(None, "gx", "gy"),
        P(None, "gx", "gy"),
        P("gx", "gy"),
        P("gx", "gy"),
        P("gx", "gy"),
    )
    out_specs = (P(None, "gx", "gy"), P(None, "gx", "gy"), P(None, "gx", "gy"))
    return jax.shard_map(body, mesh=mesh, in_specs=in_specs, out_specs=out_specs, check_vma=False)
```

```python
import jax
import jax.numpy as jnp
from jax import lax
from jax.experimental import pallas as pl
from jax.experimental.pallas import tpu as pltpu
from jax.sharding import PartitionSpec as P

CX = 4
CY = 16
NZ = 64
MIG = 256
CORNER = 64
PAIR = 2 * CORNER
WIDE = MIG + PAIR
YY = 20
YP = 24
Y_ROWS = 104
Y_STATES = 48
X_ROWS = 160
X_STATES = 112
time_step = 0.1
gravity = 1.0
mass_floor = 0.5
STEPS = (-1, 0, 1)
F32 = jnp.float32
BF16 = jnp.bfloat16


def spline(offset):
    low = 0.5 - offset
    high = 0.5 + offset
    return (0.5 * (low * low), 0.75 - offset * offset, 0.5 * (high * high))


def deposit_terms(state, living):
    mass = state[15] * living
    affine = [mass * state[6 + j] for j in range(9)]
    carried = []
    for i in range(3):
        skew = affine[3 * i] * state[0] + affine[3 * i + 1] * state[1] + affine[3 * i + 2] * state[2]
        carried.append(mass * state[3 + i] - skew)
    return mass, carried, affine


def placed(rows, width, cell, weights, row=None):
    if row is None:
        row = lax.broadcasted_iota(jnp.int32, (rows, width), 0)
    step = row - cell
    low, mid, high = weights
    zero = jnp.zeros((rows, width), F32)
    is_low, is_high = step == -1, step == 1
    moment = jnp.where(is_low, -low, jnp.where(is_high, high, zero))
    plain = jnp.where(is_low, low, jnp.where(is_high, high, jnp.where(step == 0, mid, zero)))
    return plain, moment


def split(value):
    coarse = value.astype(BF16)
    fine = (value - coarse.astype(F32)).astype(BF16)
    return coarse, fine


def low_half(shape):
    return lax.broadcasted_iota(jnp.int32, shape, len(shape) - 1) % 128 < NZ


def swap_half(value):
    return pltpu.roll(value, NZ, value.ndim - 1)


def scatter_product(lhs, depth_plain, depth_moment):
    rhs = jnp.concatenate([depth_plain, depth_moment], axis=1)
    rhs = jnp.concatenate(split(rhs), axis=0)
    rows = lhs.shape[0]
    product = lax.dot_general(
        jnp.concatenate(split(lhs), axis=0), rhs, (((1,), (1,)), ((), ())), preferred_element_type=F32
    )
    return product[0:rows] + product[rows : 2 * rows]


def row_of(value, g):
    return value[g : g + 1, :]


def join_pairs(value, first, second):
    return jnp.concatenate([value[first : first + 1, :], value[second : second + 1, :]], axis=1)


def fold_pair(first, second):
    low = low_half(first.shape)
    return jnp.where(low, first, second) + swap_half(jnp.where(low, second, first))


def resident_living(count_ref, y):
    lane = 128 * (y // 2)
    counts = count_ref[:, lane : lane + 128]
    low = low_half(counts.shape)
    if y % 2 == 0:
        counts = jnp.where(low, counts, swap_half(counts))
    else:
        counts = jnp.where(low, swap_half(counts), counts)
    counts = jnp.concatenate([counts, counts], axis=0)
    row = lax.broadcasted_iota(jnp.int32, (8, 128), 0)
    lane_id = lax.broadcasted_iota(jnp.int32, (8, 128), 1)
    slot = 2 * (row // CX) + lane_id // NZ
    return (slot < counts).astype(F32)


def deposit_residents(res_ref, count_ref, terms_ref, shift_ref, total_ref, first, last):
    row = lax.broadcasted_iota(jnp.int32, (8, 128), 0)
    for y in range(first, last):
        state = [res_ref[c, y] for c in range(16)]
        mass, carried, affine = deposit_terms(state, resident_living(count_ref, y))
        stored = [mass] + carried + affine
        for axis in range(3):
            stored += list(spline(state[axis]))
        for k, value in enumerate(stored):
            terms_ref[y, k] = value
    for ex in STEPS:
        sums = {}

        def finish_node(node):
            for c in range(4):
                value = (
                    sums.pop((node, c, 0))
                    + pltpu.roll(sums.pop((node, c, 1)), 1, 1)
                    + pltpu.roll(sums.pop((node, c, -1)), 127, 1)
                )
                at = (node + 2) * 8
                shift_ref[ex + 1, c, at : at + 8, :] = value

        for y in range(first, last):
            term = [terms_ref[y, k] for k in range(13)]
            weight_x = terms_ref[y, 13 + ex + 1]
            weight_y = [terms_ref[y, 16 + k] for k in range(3)]
            along = [term[0]]
            for i in range(3):
                value = term[1 + i]
                if ex != 0:
                    value = value + term[4 + 3 * i] if ex > 0 else value - term[4 + 3 * i]
                along.append(value)
            for ez in STEPS:
                weight = weight_x * terms_ref[y, 19 + ez + 1]
                for c in range(4):
                    value = along[c]
                    if c > 0 and ez != 0:
                        lift = term[4 + 3 * (c - 1) + 2]
                        value = value + lift if ez > 0 else value - lift
                    value = weight * value
                    parts = [value, value, value]
                    if c > 0:
                        lean = weight * term[4 + 3 * (c - 1) + 1]
                        parts = [value - lean, value, value + lean]
                    for ey in STEPS:
                        key = (y + ey, c, ez)
                        part = weight_y[ey + 1] * parts[ey + 1]
                        sums[key] = sums[key] + part if key in sums else part
            finish_node(y - 1)
        finish_node(last - 1)
        finish_node(last)
    for node in range(first - 1, last + 1):
        at = (node + 2) * 8
        for c in range(4):
            value = total_ref[c, at : at + 8, :]
            for ex in STEPS:
                low = at - 2 - ex
                both = shift_ref[ex + 1, c, low : low + 8, :] + shift_ref[ex + 1, c, low + 4 : low + 12, :]
                value = value + jnp.where((row >= 2 + ex) & (row < 2 + ex + CX), both, 0.0)
            total_ref[c, at : at + 8, :] = value


def decode(cells):
    number = cells.astype(jnp.int32)
    living = (number >= 0).astype(F32)
    return living, number // (CY * NZ), (number // NZ) % CY, number % NZ


def deposit_wide(state, cells, total_ref, row_nodes, chunks):
    rows = len(row_nodes)
    living, _, cell_y, cell_z = decode(cells)
    lane = lax.broadcasted_iota(jnp.int32, (2, WIDE), 1)
    cell_y = cell_y + jnp.where(lane < MIG, 2, jnp.where(lane < MIG + CORNER, 2 + CY, 2 - CY))
    mass, carried, affine = deposit_terms(state, living)
    weights = [spline(state[axis]) for axis in range(3)]
    row = lax.broadcasted_iota(jnp.int32, (rows, WIDE), 0)
    node = row
    for k in range(rows):
        if k == 0:
            node = row + row_nodes[0]
        elif row_nodes[k] != row_nodes[k - 1] + 1:
            node = jnp.where(row >= k, row + (row_nodes[k] - k), node)
    for g in range(2):
        depth = placed(NZ, WIDE, row_of(cell_z, g), [row_of(w, g) for w in weights[2]])
        across, across_moment = placed(
            rows, WIDE, row_of(cell_y, g), [row_of(w, g) for w in weights[1]], row=node
        )
        lines = []
        zero = jnp.zeros((rows, WIDE), F32)
        for c in range(4):
            for e in STEPS:
                weight = row_of(weights[0][e + 1], g)
                if c == 0:
                    plain, moment = (weight * row_of(mass, g)) * across, zero
                else:
                    base = row_of(carried[c - 1], g) + e * row_of(affine[3 * (c - 1)], g)
                    plain = (weight * base) * across + (
                        weight * row_of(affine[3 * (c - 1) + 1], g)
                    ) * across_moment
                    moment = (weight * row_of(affine[3 * (c - 1) + 2], g)) * across
                lines.append(jnp.concatenate([plain, moment], axis=1))
        product = scatter_product(jnp.concatenate(lines, axis=0), *depth)
        for c in range(4):
            for e in STEPS:
                row = (CX if g == 0 else -1) + e + 2
                for start, count in chunks:
                    at = (3 * c + e + 1) * rows + start
                    total_ref[c, pl.ds(row_nodes[start] * 8 + row, count, stride=8), :] += product[
                        at : at + count, :
                    ]


def open_kernel(mark_ref):
    mark_ref[...] = jnp.zeros_like(mark_ref)


def leave_kernel(mark_ref, count_ref, outbox_ref, corner_ref, face_cell_ref, corner_cell_ref,
                 total_ref, stage_ref, ahead_ref, wide_ref):
    total_ref[...] = jnp.zeros_like(total_ref)

    def count(k, width):
        return jnp.broadcast_to(count_ref[0:1, k : k + 1], (4, width))

    def living_of(width, offset):
        slot = lax.broadcasted_iota(jnp.int32, (4, width), 1)
        row = lax.broadcasted_iota(jnp.int32, (4, width), 0)
        counts = jnp.where(
            row < 2,
            jnp.where(row == 0, count(offset, width), count(offset + 1, width)),
            jnp.where(row == 2, count(offset + 2, width), count(offset + 3, width)),
        )
        return slot < counts

    face_cells = jnp.where(living_of(MIG, 0), face_cell_ref[...], -1).astype(F32)
    corner_cells = jnp.where(living_of(CORNER, 4), corner_cell_ref[...], -1).astype(F32)

    faces = [outbox_ref[c] for c in range(16)]
    corners = [corner_ref[c] for c in range(16)]

    for c, (face, corner) in enumerate(zip(faces + [face_cells], corners + [corner_cells])):
        for side in range(2):
            pair = join_pairs(corner, side, side + 2)
            if c < 16:
                stage_ref[side, c : 1 + c, :] = face[2 + side : 3 + side, 0:128]
                stage_ref[side, 16 + c : 17 + c, :] = face[2 + side : 3 + side, 128:256]
                stage_ref[side, 32 + c : 33 + c, :] = pair
                ahead_ref[side, c : c + 1, :] = face[side : side + 1, 0:128]
                ahead_ref[side, 16 + c : 17 + c, :] = face[side : side + 1, 128:256]
            else:
                stage_ref[side, 48:49, :] = face[2 + side : 3 + side, 0:128]
                stage_ref[side, 49:50, :] = face[2 + side : 3 + side, 128:256]
                stage_ref[side, 50:51, :] = pair
                stage_ref[side, 51:56, :] = jnp.zeros((5, 128), F32)
                ahead_ref[side, 32:33, :] = face[side : side + 1, 0:128]
                ahead_ref[side, 33:34, :] = face[side : side + 1, 128:256]
                ahead_ref[side, 34:40, :] = jnp.zeros((6, 128), F32)

    def wide(face, corner):
        pairs = jnp.concatenate([join_pairs(corner, 0, 1), join_pairs(corner, 2, 3)], axis=0)
        return jnp.concatenate([face[0:2, :], pairs], axis=1)

    state = [wide(faces[c], corners[c]) for c in range(16)] + [wide(face_cells, corner_cells)]
    for c, value in enumerate(state):
        wide_ref[c] = value
    deposit_wide(
        state[:16], state[16], total_ref, [0, 1, 2, 17, 18, 19, 100, 101], [(0, 3), (3, 3)]
    )

    state = [face[2:4, :] for face in faces]
    living, cell_x, _, cell_z = decode(face_cells[2:4, :])
    mass, carried, affine = deposit_terms(state, living)
    weights = [spline(state[axis]) for axis in range(3)]
    for g in range(2):
        depth = placed(NZ, MIG, row_of(cell_z, g), [row_of(w, g) for w in weights[2]])
        across, across_moment = placed(8, MIG, row_of(cell_x, g) + 2, [row_of(w, g) for w in weights[0]])
        lines = []
        zero = jnp.zeros((8, MIG), F32)
        for c in range(4):
            for e in STEPS:
                weight = row_of(weights[1][e + 1], g)
                if c == 0:
                    plain, moment = (weight * row_of(mass, g)) * across, zero
                else:
                    base = row_of(carried[c - 1], g) + e * row_of(affine[3 * (c - 1) + 1], g)
                    plain = (weight * base) * across + (
                        weight * row_of(affine[3 * (c - 1)], g)
                    ) * across_moment
                    moment = (weight * row_of(affine[3 * (c - 1) + 2], g)) * across
                lines.append(jnp.concatenate([plain, moment], axis=1))
        product = scatter_product(jnp.concatenate(lines, axis=0), *depth)
        for c in range(4):
            for e in STEPS:
                at = ((CY if g == 0 else -1) + e + 2) * 8
                line = (3 * c + e + 1) * 8
                total_ref[c, at : at + 8, :] += product[line : line + 8, :]


def edge_kernel(res_ref, cells_ref, states_ref, before_ref, msg0_ref, msg1_ref, total_ref,
                terms_ref, shift_ref, stage_ref):
    total_ref[...] = before_ref[...]
    deposit_residents(res_ref, cells_ref, terms_ref, shift_ref, total_ref, 0, 2)
    deposit_residents(res_ref, cells_ref, terms_ref, shift_ref, total_ref, CY - 2, CY)

    for side in range(2):
        for pair in range(2):
            for j in range(3):
                at = ((CY + 1 + j) if side == 0 else j) * 8
                stage_ref[side, (3 * pair + j) * 8 : (3 * pair + j + 1) * 8, :] = fold_pair(
                    total_ref[2 * pair, at : at + 8, :], total_ref[2 * pair + 1, at : at + 8, :]
                )
    parity = lax.axis_index("gy") % 2
    for msg_ref, side in ((msg0_ref, parity), (msg1_ref, 1 - parity)):
        msg_ref[0:Y_STATES, :] = stage_ref[side]
        msg_ref[Y_STATES:Y_ROWS, :] = states_ref[side]


def inner_kernel(res_ref, cells_ref, before_ref, wide_ref, grid_ref, total_ref, terms_ref, shift_ref):
    total_ref[...] = before_ref[...]
    deposit_wide(
        [wide_ref[c] for c in range(16)], wide_ref[16], total_ref, list(range(3, 19)), [(0, 14)]
    )
    deposit_residents(res_ref, cells_ref, terms_ref, shift_ref, total_ref, 2, CY - 2)
    for pair in range(2):
        for yy in range(YY):
            at = yy * 8
            grid_ref[pair, at : at + 8, :] = fold_pair(
                total_ref[2 * pair, at : at + 8, :], total_ref[2 * pair + 1, at : at + 8, :]
            )


def turn_kernel(grid_ref, in1_ref, in0_ref, ahead_ref, joined_ref, msg0_ref, msg1_ref, got_ref, stage_ref):
    parity = lax.axis_index("gy") % 2
    got_ref[parity] = in1_ref[...]
    got_ref[1 - parity] = in0_ref[...]
    joined_ref[...] = grid_ref[...]
    for pair in range(2):
        for j in range(3):
            line = (3 * pair + j) * 8
            for side, yy in ((0, 1 + j), (1, CY + j)):
                joined_ref[pair, yy * 8 : yy * 8 + 8, :] += got_ref[side, line : line + 8, :]
    low = low_half((16, 128))
    for side in range(2):
        for pair in range(2):
            for j in range(3):
                row = (5 + j) if side == 0 else j
                at = (3 * pair + j) * 18
                stage_ref[side, at : at + 18, :] = joined_ref[pair, pl.ds(8 + row, 18, stride=8), :]
        stage_ref[side, X_STATES : X_STATES + 32, :] = ahead_ref[side, 0:32, :]
        from_below, from_above = got_ref[0, 80:96, :], got_ref[1, 80:96, :]
        cell_below, cell_above = got_ref[0, 96:104, :], got_ref[1, 96:104, :]
        if side == 0:
            states = jnp.where(low, from_below, swap_half(from_above))
            cells = jnp.where(low[0:8], cell_below, swap_half(cell_above))
        else:
            states = jnp.where(low, swap_half(from_below), from_above)
            cells = jnp.where(low[0:8], swap_half(cell_below), cell_above)
        stage_ref[side, X_STATES + 32 : X_STATES + 48, :] = states
        stage_ref[side, 108:110, :] = ahead_ref[side, 32:34, :]
        stage_ref[side, 110:111, :] = cells[2:3, :]
        stage_ref[side, 111:112, :] = jnp.zeros((1, 128), F32)
    parity = lax.axis_index("gx") % 2
    msg0_ref[...] = stage_ref[parity]
    msg1_ref[...] = stage_ref[1 - parity]


def both(first, second):
    return jnp.concatenate([first, second], axis=0)


def split_depth(depth_plain, depth_moment):
    return split(jnp.concatenate([depth_plain, depth_moment], axis=1))


def gather_product(nodes, coarse_depth, fine_depth):
    low = low_half(nodes.shape)
    coarse = nodes.astype(BF16).astype(F32)
    lhs = jnp.where(low, coarse, nodes - coarse).astype(BF16)
    dims = (((1,), (0,)), ((), ()))
    return lax.dot_general(lhs, both(coarse_depth, coarse_depth), dims, preferred_element_type=F32) + (
        lax.dot_general(lhs, both(fine_depth, fine_depth), dims, preferred_element_type=F32)
    )


def contract(product, rows, width, normal, across, across_moment, normal_axis, across_axis):
    velocity, slopes = [], []
    for i in range(3):
        plain = [product[(3 * i + k) * rows : (3 * i + k + 1) * rows, 0:width] for k in range(3)]
        lifted = [
            product[(3 * i + k) * rows : (3 * i + k + 1) * rows, width : 2 * width] for k in range(3)
        ]
        low, mid, high = [normal[k] * plain[k] for k in range(3)]
        summed = low + mid + high
        stepped = high - low
        raised = normal[0] * lifted[0] + normal[1] * lifted[1] + normal[2] * lifted[2]
        velocity.append(jnp.sum(across * summed, axis=0, keepdims=True))
        slope = [None, None, jnp.sum(across * raised, axis=0, keepdims=True)]
        slope[normal_axis] = jnp.sum(across * stepped, axis=0, keepdims=True)
        slope[across_axis] = jnp.sum(across_moment * summed, axis=0, keepdims=True)
        slopes.append(slope)
    return velocity, slopes


def finished(state, living, velocity, slopes):
    out = [living * state[k] + (0.25 * time_step) * velocity[k] for k in range(3)]
    out += [0.25 * velocity[k] for k in range(3)]
    for i in range(3):
        out += [slopes[i][k] - state[k] * velocity[i] for k in range(3)]
    return out + [living * state[15]]


def rows_of(got_ref, lines):
    return jnp.concatenate([both(got_ref[0, a : a + 1, :], got_ref[1, a : a + 1, :]) for a in lines], axis=1)


def prepared(got_ref, lines, cell_lines):
    state = [rows_of(got_ref, [a + c for a in lines]) for c in range(16)]
    number = rows_of(got_ref, cell_lines).astype(jnp.int32)
    living = (number >= 0).astype(F32)
    weights = [spline(state[axis]) for axis in range(3)]
    return state, number, living, weights


def laid_out(side, rows, width, number, across_cell, depth_weights, across_weights):
    depth = placed(NZ, width, row_of(number % NZ, side), [row_of(w, side) for w in depth_weights])
    across = placed(rows, width, row_of(across_cell, side), [row_of(w, side) for w in across_weights])
    return split_depth(*depth), across


def ready_kernel(res_ref, cells_ref, y1_ref, y0_ref, weights_ref, rows_ref, depth_ref, across_ref, got_ref):
    parity = lax.axis_index("gy") % 2
    got_ref[parity] = y1_ref[...]
    got_ref[1 - parity] = y0_ref[...]
    state, number, living, weights = prepared(got_ref, (48, 64), (96, 97))
    for c in range(16):
        rows_ref[c] = state[c]
    rows_ref[16] = living
    for k in range(3):
        rows_ref[17 + k] = 4.0 * living * weights[1][k]
    for side in range(2):
        depth, across = laid_out(side, 8, MIG, number, number // (CY * NZ) + 2, weights[2], weights[0])
        for k in range(2):
            depth_ref[side, k] = depth[k]
            across_ref[side, k] = across[k]
    for y in range(CY):
        living = resident_living(cells_ref, y)
        weights = [spline(res_ref[axis, y]) for axis in range(3)]
        scale = 4.0 * living
        for k in range(3):
            weights_ref[y, k] = scale * weights[0][k]
            weights_ref[y, 3 + k] = weights[1][k]
            weights_ref[y, 6 + k] = weights[2][k]
        weights_ref[y, 9] = living


def last_kernel(res_ref, joined_ref, weights_ref, rows_ref, depth_ref, across_ref, x1_ref, x0_ref,
                out_hbm, face_out_hbm, corner_out_hbm, got_x_ref, grid_ref, vel_ref, near_ref,
                out_ref, face_out_ref, corner_out_ref, sems):
    parity = lax.axis_index("gx") % 2
    got_x_ref[parity] = x1_ref[...]
    got_x_ref[1 - parity] = x0_ref[...]

    grid_ref[...] = joined_ref[...]
    for side in range(2):
        for pair in range(2):
            for j in range(3):
                row = (1 + j) if side == 0 else (4 + j)
                at = (3 * pair + j) * 18
                grid_ref[pair, pl.ds(8 + row, 18, stride=8), :] += got_x_ref[side, at : at + 18, :]

    vel_ref[...] = jnp.zeros_like(vel_ref)
    low = low_half((8, 128))
    row = lax.broadcasted_iota(jnp.int32, (8, 128), 0)
    layer = lax.broadcasted_iota(jnp.int32, (8, 128), 1) % NZ
    inside = (layer > 0) & (layer < NZ - 1)
    upper = row < CX
    for yy in range(1, CY + 3):
        first = grid_ref[0, yy * 8 : yy * 8 + 8, :]
        second = grid_ref[1, yy * 8 : yy * 8 + 8, :]
        first_swap, second_swap = swap_half(first), swap_half(second)
        share = 1.0 / (0.25 * jnp.maximum(jnp.where(low, first, first_swap), mass_floor))
        momentum = (
            jnp.where(low, first_swap, first),
            jnp.where(low, second, second_swap),
            jnp.where(low, second_swap, second),
        )
        for i in range(3):
            value = (0.25 * momentum[i]) * share
            if i == 2:
                value = value - time_step * gravity
            vel_ref[i, yy * 8 : yy * 8 + 8, :] = jnp.where(inside, value, 0.0)
    for yy in range(1, CY + 3):
        for i in range(3):
            for ex in STEPS:
                at = yy * 8 + ex
                near = jnp.where(upper, vel_ref[i, at + 2 : at + 10, :], vel_ref[i, at - 2 : at + 6, :])
                near_ref[ex + 1, 1, i, yy - 1] = near
                near_ref[ex + 1, 0, i, yy - 1] = pltpu.roll(near, 1, 1)
                near_ref[ex + 1, 2, i, yy - 1] = pltpu.roll(near, 127, 1)

    copies = []
    for y in range(CY):
        state = [res_ref[c, y] if c < 3 or c == 15 else None for c in range(16)]
        living = weights_ref[y, 9]
        weights = [[weights_ref[y, 3 * axis + k] for k in range(3)] for axis in range(3)]
        velocity, slopes = [], []
        for i in range(3):
            by_x = []
            for kx in range(3):
                by_y = []
                for ky in range(3):
                    low_z, mid_z, high_z = [
                        weights[2][kz] * near_ref[kx, kz, i, y + ky] for kz in range(3)
                    ]
                    by_y.append((low_z + mid_z + high_z, high_z - low_z))
                low_y, mid_y, high_y = [weights[1][k] * by_y[k][0] for k in range(3)]
                raised = (
                    weights[1][0] * by_y[0][1] + weights[1][1] * by_y[1][1] + weights[1][2] * by_y[2][1]
                )
                by_x.append((low_y + mid_y + high_y, high_y - low_y, raised))
            low_x, mid_x, high_x = [weights[0][k] * by_x[k][0] for k in range(3)]
            velocity.append(low_x + mid_x + high_x)
            slope = [high_x - low_x]
            for part in (1, 2):
                slope.append(
                    weights[0][0] * by_x[0][part]
                    + weights[0][1] * by_x[1][part]
                    + weights[0][2] * by_x[2][part]
                )
            slopes.append(slope)
        for c, value in enumerate(finished(state, living, velocity, slopes)):
            out_ref[c, y] = value
        if y % 4 == 3:
            copies.append(
                pltpu.make_async_copy(
                    out_ref.at[:, y - 3 : y + 1], out_hbm.at[:, y - 3 : y + 1], sems.at[y // 4]
                )
            )
            copies[-1].start()

    def joined_sides(parts):
        velocity = [both(parts[0][0][i], parts[1][0][i]) for i in range(3)]
        slopes = [[both(parts[0][1][i][k], parts[1][1][i][k]) for k in range(3)] for i in range(3)]
        return velocity, slopes

    state, number, living, weights = prepared(
        got_x_ref, (X_STATES, X_STATES + 16, X_STATES + 32), (108, 109, 110)
    )
    scale = 4.0 * living
    parts = []
    for side in range(2):
        depth, across = laid_out(
            side, YP, WIDE, number, (number // NZ) % CY + 2, weights[2], weights[1]
        )
        first = (0 if side == 0 else CX - 1) + 2
        nodes = [vel_ref[i, pl.ds(first + e, YP, stride=8), :] for i in range(3) for e in STEPS]
        product = gather_product(jnp.concatenate(nodes, axis=0), *depth)
        normal = [row_of(scale * value, side) for value in weights[0]]
        parts.append(contract(product, YP, WIDE, normal, *across, 0, 1))
    for c, value in enumerate(finished(state, living, *joined_sides(parts))):
        face_out_ref[c, 0:2, :] = value[:, 0:MIG]
        for side in range(2):
            corner_out_ref[c, 2 * side : 2 * side + 1, :] = row_of(value, side)[:, MIG : MIG + CORNER]
            corner_out_ref[c, 2 * side + 1 : 2 * side + 2, :] = row_of(value, side)[:, MIG + CORNER : WIDE]

    state = [rows_ref[c] for c in range(16)]
    living = rows_ref[16]
    parts = []
    for side in range(2):
        first = (0 if side == 0 else CY - 1) + 2
        nodes = [
            vel_ref[i, (first + e) * 8 : (first + e) * 8 + 8, :] for i in range(3) for e in STEPS
        ]
        product = gather_product(jnp.concatenate(nodes, axis=0), depth_ref[side, 0], depth_ref[side, 1])
        normal = [row_of(rows_ref[17 + k], side) for k in range(3)]
        parts.append(contract(product, 8, MIG, normal, across_ref[side, 0], across_ref[side, 1], 1, 0))
    for c, value in enumerate(finished(state, living, *joined_sides(parts))):
        face_out_ref[c, 2:4, :] = value

    copies.append(pltpu.make_async_copy(face_out_ref, face_out_hbm, sems.at[4]))
    copies.append(pltpu.make_async_copy(corner_out_ref, corner_out_hbm, sems.at[5]))
    for copy in copies[-2:]:
        copy.start()
    for copy in copies:
        copy.wait()


def partner(index, phase, count):
    return (((index - phase) % count ^ 1) + phase) % count


def swapped(value, axis, phase):
    count = lax.axis_size(axis)
    return lax.ppermute(value, axis, [(i, partner(i, phase, count)) for i in range(count)])


VMEM = pl.BlockSpec(memory_space=pltpu.VMEM)
HBM = pl.BlockSpec(memory_space=pltpu.HBM)


def scratch(shape, dtype=F32):
    return pltpu.VMEM(shape, dtype)


def call(kernel, in_specs, out_spec, out_shapes, scratch_shapes, flops):
    return pl.pallas_call(
        kernel,
        in_specs=in_specs,
        out_specs=[out_spec] * len(out_shapes),
        out_shape=[
            jax.ShapeDtypeStruct(shape[:-1], BF16) if shape[-1] is BF16 else jax.ShapeDtypeStruct(shape, F32)
            for shape in out_shapes
        ],
        scratch_shapes=scratch_shapes,
        compiler_params=pltpu.CompilerParams(vmem_limit_bytes=24 * 1024 * 1024),
        cost_estimate=pl.CostEstimate(flops=flops, bytes_accessed=1 << 20, transcendentals=0),
    )


def body(residents, cell_count, outbox, corner_box, face_cell, corner_cell, mig_count):
    res = residents.reshape(16, CX, CY, 2, 128).transpose(0, 2, 3, 1, 4).reshape(16, CY, 8, 128)
    (mark,) = call(open_kernel, [], VMEM, [(8, 128)], [], 10_000_000_000)()
    left, states, ahead, wide = call(
        leave_kernel,
        [VMEM] * 6,
        VMEM,
        [(4, YP * 8, 128), (2, Y_ROWS - Y_STATES, 128), (2, 40, 128), (17, 2, WIDE)],
        [],
        10_000_000,
    )(mark, mig_count.reshape(1, 8), outbox, corner_box, face_cell, corner_cell)
    msg0, msg1, total = call(
        edge_kernel,
        [VMEM] * 4,
        VMEM,
        [(Y_ROWS, 128), (Y_ROWS, 128), (4, YP * 8, 128)],
        [scratch((CY, 22, 8, 128)), scratch((3, 4, YP * 8, 128)), scratch((2, Y_STATES, 128))],
        10_000_000,
    )(res, cell_count, states, left)
    y0 = swapped(msg0, "gy", 0)
    y1 = swapped(msg1, "gy", 1)
    (grid,) = call(
        inner_kernel,
        [VMEM] * 4,
        VMEM,
        [(2, YY * 8, 128)],
        [scratch((4, YP * 8, 128)), scratch((CY, 22, 8, 128)), scratch((3, 4, YP * 8, 128))],
        10_000_000,
    )(res, cell_count, total, wide)
    joined, msg0, msg1 = call(
        turn_kernel,
        [VMEM] * 4,
        VMEM,
        [(2, YY * 8, 128), (X_ROWS, 128), (X_ROWS, 128)],
        [scratch((2, Y_ROWS, 128)), scratch((2, X_ROWS, 128))],
        1_000_000,
    )(grid, y1, y0, ahead)
    x0 = swapped(msg0, "gx", 0)
    x1 = swapped(msg1, "gx", 1)
    weights, rows, depth, across = call(
        ready_kernel,
        [VMEM] * 4,
        VMEM,
        [(CY, 10, 8, 128), (20, 2, MIG), (2, 2, NZ, 2 * MIG, BF16), (2, 2, 8, MIG)],
        [scratch((2, Y_ROWS, 128))],
        10_000_000,
    )(res, cell_count, y1, y0)
    out, face_out, corner_out = call(
        last_kernel,
        [VMEM] * 8,
        HBM,
        [(16, CY, 8, 128), (16, 4, MIG), (16, 4, CORNER)],
        [
            scratch((2, X_ROWS, 128)),
            scratch((2, YY * 8, 128)),
            scratch((3, YP * 8, 128)),
            scratch((3, 3, 3, CY + 2, 8, 128)),
            scratch((16, CY, 8, 128)),
            scratch((16, 4, MIG)),
            scratch((16, 4, CORNER)),
            pltpu.SemaphoreType.DMA((6,)),
        ],
        10_000_000,
    )(res, joined, weights, rows, depth, across, x1, x0)
    out = out.reshape(16, CY, 2, CX, 128).transpose(0, 3, 1, 2, 4).reshape(16, CX, CY * 256)
    return out, face_out, corner_out


def solution(mesh):
    in_specs = (
        P(None, "gx", "gy"),
        P("gx", "gy"),
        P(None, "gx", "gy"),
        P(None, "gx", "gy"),
        P("gx", "gy"),
        P("gx", "gy"),
        P("gx", "gy"),
    )
    out_specs = (P(None, "gx", "gy"), P(None, "gx", "gy"), P(None, "gx", "gy"))
    return jax.shard_map(body, mesh=mesh, in_specs=in_specs, out_specs=out_specs, check_vma=False)
```

```python
import jax
import jax.numpy as jnp
from jax import lax
from jax.experimental import pallas as pl
from jax.experimental.pallas import tpu as pltpu
from jax.sharding import PartitionSpec as P

CX = 4
CY = 16
NZ = 64
MIG = 256
CORNER = 64
PAIR = 2 * CORNER
WIDE = MIG + PAIR
YY = 20
YP = 24
Y_ROWS = 104
Y_STATES = 48
X_ROWS = 160
X_STATES = 112
time_step = 0.1
gravity = 1.0
mass_floor = 0.5
STEPS = (-1, 0, 1)
F32 = jnp.float32
BF16 = jnp.bfloat16


def spline(offset):
    low = 0.5 - offset
    high = 0.5 + offset
    return (0.5 * (low * low), 0.75 - offset * offset, 0.5 * (high * high))


def deposit_terms(state, living):
    mass = state[15] * living
    affine = [mass * state[6 + j] for j in range(9)]
    carried = []
    for i in range(3):
        skew = affine[3 * i] * state[0] + affine[3 * i + 1] * state[1] + affine[3 * i + 2] * state[2]
        carried.append(mass * state[3 + i] - skew)
    return mass, carried, affine


def placed(rows, width, cell, weights, row=None):
    if row is None:
        row = lax.broadcasted_iota(jnp.int32, (rows, width), 0)
    step = row - cell
    low, mid, high = weights
    zero = jnp.zeros((rows, width), F32)
    is_low, is_high = step == -1, step == 1
    moment = jnp.where(is_low, -low, jnp.where(is_high, high, zero))
    plain = jnp.where(is_low, low, jnp.where(is_high, high, jnp.where(step == 0, mid, zero)))
    return plain, moment


def placed_depth(width, cell, weights):
    row = lax.broadcasted_iota(jnp.int32, (NZ, width), 0).astype(F32).astype(BF16)
    step = row - jnp.broadcast_to(cell.astype(F32).astype(BF16), (NZ, width))
    is_low, is_mid, is_high = step == -1.0, step == 0.0, step == 1.0
    zero = jnp.zeros((NZ, width), BF16)
    parts = []
    for low, mid, high in zip(*[split(value) for value in weights]):
        low, mid, high = [jnp.broadcast_to(value, (NZ, width)) for value in (low, mid, high)]
        moment = jnp.where(is_low, -low, jnp.where(is_high, high, zero))
        plain = jnp.where(is_low, low, jnp.where(is_high, high, jnp.where(is_mid, mid, zero)))
        parts.append(jnp.concatenate([plain, moment], axis=1))
    return parts


def split(value):
    coarse = value.astype(BF16)
    fine = (value - coarse.astype(F32)).astype(BF16)
    return coarse, fine


def low_half(shape):
    return lax.broadcasted_iota(jnp.int32, shape, len(shape) - 1) % 128 < NZ


def swap_half(value):
    return pltpu.roll(value, NZ, value.ndim - 1)


def scatter_product(lhs, coarse_depth, fine_depth):
    rhs = jnp.concatenate([coarse_depth, fine_depth], axis=0)
    rows = lhs.shape[0]
    product = lax.dot_general(
        jnp.concatenate(split(lhs), axis=0), rhs, (((1,), (1,)), ((), ())), preferred_element_type=F32
    )
    return product[0:rows] + product[rows : 2 * rows]


def row_of(value, g):
    return value[g : g + 1, :]


def join_pairs(value, first, second):
    return jnp.concatenate([value[first : first + 1, :], value[second : second + 1, :]], axis=1)


def fold_pair(first, second):
    low = low_half(first.shape)
    return jnp.where(low, first, second) + swap_half(jnp.where(low, second, first))


def resident_living(count_ref, y):
    lane = 128 * (y // 2)
    counts = count_ref[:, lane : lane + 128]
    low = low_half(counts.shape)
    if y % 2 == 0:
        counts = jnp.where(low, counts, swap_half(counts))
    else:
        counts = jnp.where(low, swap_half(counts), counts)
    counts = jnp.concatenate([counts, counts], axis=0)
    row = lax.broadcasted_iota(jnp.int32, (8, 128), 0)
    lane_id = lax.broadcasted_iota(jnp.int32, (8, 128), 1)
    slot = 2 * (row // CX) + lane_id // NZ
    return (slot < counts).astype(F32)


def deposit_residents(res_ref, count_ref, terms_ref, shift_ref, total_ref, first, last):
    row = lax.broadcasted_iota(jnp.int32, (8, 128), 0)
    for y in range(first, last):
        state = [res_ref[c, y] for c in range(16)]
        mass, carried, affine = deposit_terms(state, resident_living(count_ref, y))
        stored = [mass] + carried + affine
        for axis in range(3):
            stored += list(spline(state[axis]))
        for k, value in enumerate(stored):
            terms_ref[y, k] = value
    for ex in STEPS:
        sums = {}

        def finish_node(node):
            for c in range(4):
                value = (
                    sums.pop((node, c, 0))
                    + pltpu.roll(sums.pop((node, c, 1)), 1, 1)
                    + pltpu.roll(sums.pop((node, c, -1)), 127, 1)
                )
                at = (node + 2) * 8
                shift_ref[ex + 1, c, at : at + 8, :] = value

        for y in range(first, last):
            term = [terms_ref[y, k] for k in range(13)]
            weight_x = terms_ref[y, 13 + ex + 1]
            weight_y = [terms_ref[y, 16 + k] for k in range(3)]
            along = [term[0]]
            for i in range(3):
                value = term[1 + i]
                if ex != 0:
                    value = value + term[4 + 3 * i] if ex > 0 else value - term[4 + 3 * i]
                along.append(value)
            for ez in STEPS:
                weight = weight_x * terms_ref[y, 19 + ez + 1]
                for c in range(4):
                    value = along[c]
                    if c > 0 and ez != 0:
                        lift = term[4 + 3 * (c - 1) + 2]
                        value = value + lift if ez > 0 else value - lift
                    value = weight * value
                    parts = [value, value, value]
                    if c > 0:
                        lean = weight * term[4 + 3 * (c - 1) + 1]
                        parts = [value - lean, value, value + lean]
                    for ey in STEPS:
                        key = (y + ey, c, ez)
                        part = weight_y[ey + 1] * parts[ey + 1]
                        sums[key] = sums[key] + part if key in sums else part
            finish_node(y - 1)
        finish_node(last - 1)
        finish_node(last)
    for node in range(first - 1, last + 1):
        at = (node + 2) * 8
        for c in range(4):
            value = total_ref[c, at : at + 8, :]
            for ex in STEPS:
                low = at - 2 - ex
                both = shift_ref[ex + 1, c, low : low + 8, :] + shift_ref[ex + 1, c, low + 4 : low + 12, :]
                value = value + jnp.where((row >= 2 + ex) & (row < 2 + ex + CX), both, 0.0)
            total_ref[c, at : at + 8, :] = value


def decode(cells):
    number = cells.astype(jnp.int32)
    living = (number >= 0).astype(F32)
    return living, number // (CY * NZ), (number // NZ) % CY, number % NZ


def deposit_wide(state, cells, total_ref, row_nodes, chunks):
    rows = len(row_nodes)
    living, _, cell_y, cell_z = decode(cells)
    lane = lax.broadcasted_iota(jnp.int32, (2, WIDE), 1)
    cell_y = cell_y + jnp.where(lane < MIG, 2, jnp.where(lane < MIG + CORNER, 2 + CY, 2 - CY))
    mass, carried, affine = deposit_terms(state, living)
    weights = [spline(state[axis]) for axis in range(3)]
    row = lax.broadcasted_iota(jnp.int32, (rows, WIDE), 0)
    node = row
    for k in range(rows):
        if k == 0:
            node = row + row_nodes[0]
        elif row_nodes[k] != row_nodes[k - 1] + 1:
            node = jnp.where(row >= k, row + (row_nodes[k] - k), node)
    for g in range(2):
        depth = placed_depth(WIDE, row_of(cell_z, g), [row_of(w, g) for w in weights[2]])
        across, across_moment = placed(
            rows, WIDE, row_of(cell_y, g), [row_of(w, g) for w in weights[1]], row=node
        )
        lines = []
        zero = jnp.zeros((rows, WIDE), F32)
        for c in range(4):
            for e in STEPS:
                weight = row_of(weights[0][e + 1], g)
                if c == 0:
                    plain, moment = (weight * row_of(mass, g)) * across, zero
                else:
                    base = row_of(carried[c - 1], g) + e * row_of(affine[3 * (c - 1)], g)
                    plain = (weight * base) * across + (
                        weight * row_of(affine[3 * (c - 1) + 1], g)
                    ) * across_moment
                    moment = (weight * row_of(affine[3 * (c - 1) + 2], g)) * across
                lines.append(jnp.concatenate([plain, moment], axis=1))
        product = scatter_product(jnp.concatenate(lines, axis=0), *depth)
        for c in range(4):
            for e in STEPS:
                row = (CX if g == 0 else -1) + e + 2
                for start, count in chunks:
                    at = (3 * c + e + 1) * rows + start
                    total_ref[c, pl.ds(row_nodes[start] * 8 + row, count, stride=8), :] += product[
                        at : at + count, :
                    ]


def open_kernel(mark_ref):
    mark_ref[...] = jnp.zeros_like(mark_ref)


def leave_kernel(mark_ref, count_ref, outbox_ref, corner_ref, face_cell_ref, corner_cell_ref,
                 total_ref, stage_ref, ahead_ref, wide_ref):
    total_ref[...] = jnp.zeros_like(total_ref)

    def count(k, width):
        return jnp.broadcast_to(count_ref[0:1, k : k + 1], (4, width))

    def living_of(width, offset):
        slot = lax.broadcasted_iota(jnp.int32, (4, width), 1)
        row = lax.broadcasted_iota(jnp.int32, (4, width), 0)
        counts = jnp.where(
            row < 2,
            jnp.where(row == 0, count(offset, width), count(offset + 1, width)),
            jnp.where(row == 2, count(offset + 2, width), count(offset + 3, width)),
        )
        return slot < counts

    face_cells = jnp.where(living_of(MIG, 0), face_cell_ref[...], -1).astype(F32)
    corner_cells = jnp.where(living_of(CORNER, 4), corner_cell_ref[...], -1).astype(F32)

    faces = [outbox_ref[c] for c in range(16)]
    corners = [corner_ref[c] for c in range(16)]

    for c, (face, corner) in enumerate(zip(faces + [face_cells], corners + [corner_cells])):
        for side in range(2):
            pair = join_pairs(corner, side, side + 2)
            if c < 16:
                stage_ref[side, c : 1 + c, :] = face[2 + side : 3 + side, 0:128]
                stage_ref[side, 16 + c : 17 + c, :] = face[2 + side : 3 + side, 128:256]
                stage_ref[side, 32 + c : 33 + c, :] = pair
                ahead_ref[side, c : c + 1, :] = face[side : side + 1, 0:128]
                ahead_ref[side, 16 + c : 17 + c, :] = face[side : side + 1, 128:256]
            else:
                stage_ref[side, 48:49, :] = face[2 + side : 3 + side, 0:128]
                stage_ref[side, 49:50, :] = face[2 + side : 3 + side, 128:256]
                stage_ref[side, 50:51, :] = pair
                stage_ref[side, 51:56, :] = jnp.zeros((5, 128), F32)
                ahead_ref[side, 32:33, :] = face[side : side + 1, 0:128]
                ahead_ref[side, 33:34, :] = face[side : side + 1, 128:256]
                ahead_ref[side, 34:40, :] = jnp.zeros((6, 128), F32)

    def wide(face, corner):
        pairs = jnp.concatenate([join_pairs(corner, 0, 1), join_pairs(corner, 2, 3)], axis=0)
        return jnp.concatenate([face[0:2, :], pairs], axis=1)

    state = [wide(faces[c], corners[c]) for c in range(16)] + [wide(face_cells, corner_cells)]
    for c, value in enumerate(state):
        wide_ref[c] = value
    deposit_wide(
        state[:16], state[16], total_ref, [0, 1, 2, 17, 18, 19, 100, 101], [(0, 3), (3, 3)]
    )

    state = [face[2:4, :] for face in faces]
    living, cell_x, _, cell_z = decode(face_cells[2:4, :])
    mass, carried, affine = deposit_terms(state, living)
    weights = [spline(state[axis]) for axis in range(3)]
    for g in range(2):
        depth = placed_depth(MIG, row_of(cell_z, g), [row_of(w, g) for w in weights[2]])
        across, across_moment = placed(8, MIG, row_of(cell_x, g) + 2, [row_of(w, g) for w in weights[0]])
        lines = []
        zero = jnp.zeros((8, MIG), F32)
        for c in range(4):
            for e in STEPS:
                weight = row_of(weights[1][e + 1], g)
                if c == 0:
                    plain, moment = (weight * row_of(mass, g)) * across, zero
                else:
                    base = row_of(carried[c - 1], g) + e * row_of(affine[3 * (c - 1) + 1], g)
                    plain = (weight * base) * across + (
                        weight * row_of(affine[3 * (c - 1)], g)
                    ) * across_moment
                    moment = (weight * row_of(affine[3 * (c - 1) + 2], g)) * across
                lines.append(jnp.concatenate([plain, moment], axis=1))
        product = scatter_product(jnp.concatenate(lines, axis=0), *depth)
        for c in range(4):
            for e in STEPS:
                at = ((CY if g == 0 else -1) + e + 2) * 8
                line = (3 * c + e + 1) * 8
                total_ref[c, at : at + 8, :] += product[line : line + 8, :]


def edge_kernel(res_ref, cells_ref, states_ref, before_ref, msg0_ref, msg1_ref, total_ref,
                terms_ref, shift_ref, stage_ref):
    total_ref[...] = before_ref[...]
    deposit_residents(res_ref, cells_ref, terms_ref, shift_ref, total_ref, 0, 2)
    deposit_residents(res_ref, cells_ref, terms_ref, shift_ref, total_ref, CY - 2, CY)

    for side in range(2):
        for pair in range(2):
            for j in range(3):
                at = ((CY + 1 + j) if side == 0 else j) * 8
                stage_ref[side, (3 * pair + j) * 8 : (3 * pair + j + 1) * 8, :] = fold_pair(
                    total_ref[2 * pair, at : at + 8, :], total_ref[2 * pair + 1, at : at + 8, :]
                )
    parity = lax.axis_index("gy") % 2
    for msg_ref, side in ((msg0_ref, parity), (msg1_ref, 1 - parity)):
        msg_ref[0:Y_STATES, :] = stage_ref[side]
        msg_ref[Y_STATES:Y_ROWS, :] = states_ref[side]


def inner_kernel(res_ref, cells_ref, before_ref, wide_ref, grid_ref, total_ref, terms_ref, shift_ref):
    total_ref[...] = before_ref[...]
    deposit_wide(
        [wide_ref[c] for c in range(16)], wide_ref[16], total_ref, list(range(3, 19)), [(0, 14)]
    )
    deposit_residents(res_ref, cells_ref, terms_ref, shift_ref, total_ref, 2, CY - 2)
    for pair in range(2):
        for yy in range(YY):
            at = yy * 8
            grid_ref[pair, at : at + 8, :] = fold_pair(
                total_ref[2 * pair, at : at + 8, :], total_ref[2 * pair + 1, at : at + 8, :]
            )


def turn_kernel(grid_ref, in1_ref, in0_ref, ahead_ref, joined_ref, msg0_ref, msg1_ref, got_ref, stage_ref):
    parity = lax.axis_index("gy") % 2
    got_ref[parity] = in1_ref[...]
    got_ref[1 - parity] = in0_ref[...]
    joined_ref[...] = grid_ref[...]
    for pair in range(2):
        for j in range(3):
            line = (3 * pair + j) * 8
            for side, yy in ((0, 1 + j), (1, CY + j)):
                joined_ref[pair, yy * 8 : yy * 8 + 8, :] += got_ref[side, line : line + 8, :]
    low = low_half((16, 128))
    for side in range(2):
        for pair in range(2):
            for j in range(3):
                row = (5 + j) if side == 0 else j
                at = (3 * pair + j) * 18
                stage_ref[side, at : at + 18, :] = joined_ref[pair, pl.ds(8 + row, 18, stride=8), :]
        stage_ref[side, X_STATES : X_STATES + 32, :] = ahead_ref[side, 0:32, :]
        from_below, from_above = got_ref[0, 80:96, :], got_ref[1, 80:96, :]
        cell_below, cell_above = got_ref[0, 96:104, :], got_ref[1, 96:104, :]
        if side == 0:
            states = jnp.where(low, from_below, swap_half(from_above))
            cells = jnp.where(low[0:8], cell_below, swap_half(cell_above))
        else:
            states = jnp.where(low, swap_half(from_below), from_above)
            cells = jnp.where(low[0:8], swap_half(cell_below), cell_above)
        stage_ref[side, X_STATES + 32 : X_STATES + 48, :] = states
        stage_ref[side, 108:110, :] = ahead_ref[side, 32:34, :]
        stage_ref[side, 110:111, :] = cells[2:3, :]
        stage_ref[side, 111:112, :] = jnp.zeros((1, 128), F32)
    parity = lax.axis_index("gx") % 2
    msg0_ref[...] = stage_ref[parity]
    msg1_ref[...] = stage_ref[1 - parity]


def both(first, second):
    return jnp.concatenate([first, second], axis=0)


def gather_product(nodes, coarse_depth, fine_depth):
    low = low_half(nodes.shape)
    coarse = nodes.astype(BF16).astype(F32)
    lhs = jnp.where(low, coarse, nodes - coarse).astype(BF16)
    dims = (((1,), (0,)), ((), ()))
    return lax.dot_general(lhs, both(coarse_depth, coarse_depth), dims, preferred_element_type=F32) + (
        lax.dot_general(lhs, both(fine_depth, fine_depth), dims, preferred_element_type=F32)
    )


def contract(product, rows, width, normal, across, across_moment, normal_axis, across_axis):
    velocity, slopes = [], []
    for i in range(3):
        plain = [product[(3 * i + k) * rows : (3 * i + k + 1) * rows, 0:width] for k in range(3)]
        lifted = [
            product[(3 * i + k) * rows : (3 * i + k + 1) * rows, width : 2 * width] for k in range(3)
        ]
        low, mid, high = [normal[k] * plain[k] for k in range(3)]
        summed = low + mid + high
        stepped = high - low
        raised = normal[0] * lifted[0] + normal[1] * lifted[1] + normal[2] * lifted[2]
        velocity.append(jnp.sum(across * summed, axis=0, keepdims=True))
        slope = [None, None, jnp.sum(across * raised, axis=0, keepdims=True)]
        slope[normal_axis] = jnp.sum(across * stepped, axis=0, keepdims=True)
        slope[across_axis] = jnp.sum(across_moment * summed, axis=0, keepdims=True)
        slopes.append(slope)
    return velocity, slopes


def finished(state, living, velocity, slopes):
    out = [living * state[k] + (0.25 * time_step) * velocity[k] for k in range(3)]
    out += [0.25 * velocity[k] for k in range(3)]
    for i in range(3):
        out += [slopes[i][k] - state[k] * velocity[i] for k in range(3)]
    return out + [living * state[15]]


def rows_of(got_ref, lines):
    return jnp.concatenate([both(got_ref[0, a : a + 1, :], got_ref[1, a : a + 1, :]) for a in lines], axis=1)


def prepared(got_ref, lines, cell_lines):
    state = [rows_of(got_ref, [a + c for a in lines]) for c in range(16)]
    number = rows_of(got_ref, cell_lines).astype(jnp.int32)
    living = (number >= 0).astype(F32)
    weights = [spline(state[axis]) for axis in range(3)]
    return state, number, living, weights


def laid_out(side, rows, width, number, across_cell, depth_weights, across_weights):
    depth = placed(NZ, width, row_of(number % NZ, side), [row_of(w, side) for w in depth_weights])
    across = placed(rows, width, row_of(across_cell, side), [row_of(w, side) for w in across_weights])
    return split(jnp.concatenate(depth, axis=1)), across


def ready_kernel(res_ref, cells_ref, y1_ref, y0_ref, weights_ref, rows_ref, depth_ref, across_ref, got_ref):
    parity = lax.axis_index("gy") % 2
    got_ref[parity] = y1_ref[...]
    got_ref[1 - parity] = y0_ref[...]
    state, number, living, weights = prepared(got_ref, (48, 64), (96, 97))
    for c in range(16):
        rows_ref[c] = state[c]
    rows_ref[16] = living
    for k in range(3):
        rows_ref[17 + k] = 4.0 * living * weights[1][k]
    for side in range(2):
        depth, across = laid_out(side, 8, MIG, number, number // (CY * NZ) + 2, weights[2], weights[0])
        for k in range(2):
            depth_ref[side, k] = depth[k]
            across_ref[side, k] = across[k]
    for y in range(CY):
        living = resident_living(cells_ref, y)
        weights = [spline(res_ref[axis, y]) for axis in range(3)]
        scale = 4.0 * living
        for k in range(3):
            weights_ref[y, k] = scale * weights[0][k]
            weights_ref[y, 3 + k] = weights[1][k]
            weights_ref[y, 6 + k] = weights[2][k]
        weights_ref[y, 9] = living


def last_kernel(res_ref, joined_ref, weights_ref, rows_ref, depth_ref, across_ref, x1_ref, x0_ref,
                out_hbm, face_out_hbm, corner_out_hbm, got_x_ref, grid_ref, vel_ref, near_ref,
                out_ref, face_out_ref, corner_out_ref, sems):
    parity = lax.axis_index("gx") % 2
    got_x_ref[parity] = x1_ref[...]
    got_x_ref[1 - parity] = x0_ref[...]

    grid_ref[...] = joined_ref[...]
    for side in range(2):
        for pair in range(2):
            for j in range(3):
                row = (1 + j) if side == 0 else (4 + j)
                at = (3 * pair + j) * 18
                grid_ref[pair, pl.ds(8 + row, 18, stride=8), :] += got_x_ref[side, at : at + 18, :]

    vel_ref[...] = jnp.zeros_like(vel_ref)
    low = low_half((8, 128))
    row = lax.broadcasted_iota(jnp.int32, (8, 128), 0)
    layer = lax.broadcasted_iota(jnp.int32, (8, 128), 1) % NZ
    inside = (layer > 0) & (layer < NZ - 1)
    upper = row < CX
    for yy in range(1, CY + 3):
        first = grid_ref[0, yy * 8 : yy * 8 + 8, :]
        second = grid_ref[1, yy * 8 : yy * 8 + 8, :]
        first_swap, second_swap = swap_half(first), swap_half(second)
        share = 1.0 / (0.25 * jnp.maximum(jnp.where(low, first, first_swap), mass_floor))
        momentum = (
            jnp.where(low, first_swap, first),
            jnp.where(low, second, second_swap),
            jnp.where(low, second_swap, second),
        )
        for i in range(3):
            value = (0.25 * momentum[i]) * share
            if i == 2:
                value = value - time_step * gravity
            vel_ref[i, yy * 8 : yy * 8 + 8, :] = jnp.where(inside, value, 0.0)
    for yy in range(1, CY + 3):
        for i in range(3):
            for ex in STEPS:
                at = yy * 8 + ex
                near = jnp.where(upper, vel_ref[i, at + 2 : at + 10, :], vel_ref[i, at - 2 : at + 6, :])
                near_ref[ex + 1, 1, i, yy - 1] = near
                near_ref[ex + 1, 0, i, yy - 1] = pltpu.roll(near, 1, 1)
                near_ref[ex + 1, 2, i, yy - 1] = pltpu.roll(near, 127, 1)

    copies = []
    for y in range(CY):
        state = [res_ref[c, y] if c < 3 or c == 15 else None for c in range(16)]
        living = weights_ref[y, 9]
        weights = [[weights_ref[y, 3 * axis + k] for k in range(3)] for axis in range(3)]
        velocity, slopes = [], []
        for i in range(3):
            by_x = []
            for kx in range(3):
                by_y = []
                for ky in range(3):
                    low_z, mid_z, high_z = [
                        weights[2][kz] * near_ref[kx, kz, i, y + ky] for kz in range(3)
                    ]
                    by_y.append((low_z + mid_z + high_z, high_z - low_z))
                low_y, mid_y, high_y = [weights[1][k] * by_y[k][0] for k in range(3)]
                raised = (
                    weights[1][0] * by_y[0][1] + weights[1][1] * by_y[1][1] + weights[1][2] * by_y[2][1]
                )
                by_x.append((low_y + mid_y + high_y, high_y - low_y, raised))
            low_x, mid_x, high_x = [weights[0][k] * by_x[k][0] for k in range(3)]
            velocity.append(low_x + mid_x + high_x)
            slope = [high_x - low_x]
            for part in (1, 2):
                slope.append(
                    weights[0][0] * by_x[0][part]
                    + weights[0][1] * by_x[1][part]
                    + weights[0][2] * by_x[2][part]
                )
            slopes.append(slope)
        for c, value in enumerate(finished(state, living, velocity, slopes)):
            out_ref[c, y] = value
        if y % 4 == 3:
            copies.append(
                pltpu.make_async_copy(
                    out_ref.at[:, y - 3 : y + 1], out_hbm.at[:, y - 3 : y + 1], sems.at[y // 4]
                )
            )
            copies[-1].start()

    def joined_sides(parts):
        velocity = [both(parts[0][0][i], parts[1][0][i]) for i in range(3)]
        slopes = [[both(parts[0][1][i][k], parts[1][1][i][k]) for k in range(3)] for i in range(3)]
        return velocity, slopes

    state, number, living, weights = prepared(
        got_x_ref, (X_STATES, X_STATES + 16, X_STATES + 32), (108, 109, 110)
    )
    scale = 4.0 * living
    parts = []
    for side in range(2):
        depth, across = laid_out(
            side, YP, WIDE, number, (number // NZ) % CY + 2, weights[2], weights[1]
        )
        first = (0 if side == 0 else CX - 1) + 2
        nodes = [vel_ref[i, pl.ds(first + e, YP, stride=8), :] for i in range(3) for e in STEPS]
        product = gather_product(jnp.concatenate(nodes, axis=0), *depth)
        normal = [row_of(scale * value, side) for value in weights[0]]
        parts.append(contract(product, YP, WIDE, normal, *across, 0, 1))
    for c, value in enumerate(finished(state, living, *joined_sides(parts))):
        face_out_ref[c, 0:2, :] = value[:, 0:MIG]
        for side in range(2):
            corner_out_ref[c, 2 * side : 2 * side + 1, :] = row_of(value, side)[:, MIG : MIG + CORNER]
            corner_out_ref[c, 2 * side + 1 : 2 * side + 2, :] = row_of(value, side)[:, MIG + CORNER : WIDE]

    state = [rows_ref[c] for c in range(16)]
    living = rows_ref[16]
    parts = []
    for side in range(2):
        first = (0 if side == 0 else CY - 1) + 2
        nodes = [
            vel_ref[i, (first + e) * 8 : (first + e) * 8 + 8, :] for i in range(3) for e in STEPS
        ]
        product = gather_product(jnp.concatenate(nodes, axis=0), depth_ref[side, 0], depth_ref[side, 1])
        normal = [row_of(rows_ref[17 + k], side) for k in range(3)]
        parts.append(contract(product, 8, MIG, normal, across_ref[side, 0], across_ref[side, 1], 1, 0))
    for c, value in enumerate(finished(state, living, *joined_sides(parts))):
        face_out_ref[c, 2:4, :] = value

    copies.append(pltpu.make_async_copy(face_out_ref, face_out_hbm, sems.at[4]))
    copies.append(pltpu.make_async_copy(corner_out_ref, corner_out_hbm, sems.at[5]))
    for copy in copies[-2:]:
        copy.start()
    for copy in copies:
        copy.wait()


def partner(index, phase, count):
    return (((index - phase) % count ^ 1) + phase) % count


def swapped(value, axis, phase):
    count = lax.axis_size(axis)
    return lax.ppermute(value, axis, [(i, partner(i, phase, count)) for i in range(count)])


VMEM = pl.BlockSpec(memory_space=pltpu.VMEM)
HBM = pl.BlockSpec(memory_space=pltpu.HBM)


def scratch(shape, dtype=F32):
    return pltpu.VMEM(shape, dtype)


def call(kernel, in_specs, out_spec, out_shapes, scratch_shapes, flops):
    return pl.pallas_call(
        kernel,
        in_specs=in_specs,
        out_specs=[out_spec] * len(out_shapes),
        out_shape=[
            jax.ShapeDtypeStruct(shape[:-1], BF16) if shape[-1] is BF16 else jax.ShapeDtypeStruct(shape, F32)
            for shape in out_shapes
        ],
        scratch_shapes=scratch_shapes,
        compiler_params=pltpu.CompilerParams(vmem_limit_bytes=24 * 1024 * 1024),
        cost_estimate=pl.CostEstimate(flops=flops, bytes_accessed=1 << 20, transcendentals=0),
    )


def body(residents, cell_count, outbox, corner_box, face_cell, corner_cell, mig_count):
    res = residents.reshape(16, CX, CY, 2, 128).transpose(0, 2, 3, 1, 4).reshape(16, CY, 8, 128)
    (mark,) = call(open_kernel, [], VMEM, [(8, 128)], [], 10_000_000_000)()
    left, states, ahead, wide = call(
        leave_kernel,
        [VMEM] * 6,
        VMEM,
        [(4, YP * 8, 128), (2, Y_ROWS - Y_STATES, 128), (2, 40, 128), (17, 2, WIDE)],
        [],
        10_000_000,
    )(mark, mig_count.reshape(1, 8), outbox, corner_box, face_cell, corner_cell)
    msg0, msg1, total = call(
        edge_kernel,
        [VMEM] * 4,
        VMEM,
        [(Y_ROWS, 128), (Y_ROWS, 128), (4, YP * 8, 128)],
        [scratch((CY, 22, 8, 128)), scratch((3, 4, YP * 8, 128)), scratch((2, Y_STATES, 128))],
        10_000_000,
    )(res, cell_count, states, left)
    y0 = swapped(msg0, "gy", 0)
    y1 = swapped(msg1, "gy", 1)
    (grid,) = call(
        inner_kernel,
        [VMEM] * 4,
        VMEM,
        [(2, YY * 8, 128)],
        [scratch((4, YP * 8, 128)), scratch((CY, 22, 8, 128)), scratch((3, 4, YP * 8, 128))],
        10_000_000,
    )(res, cell_count, total, wide)
    joined, msg0, msg1 = call(
        turn_kernel,
        [VMEM] * 4,
        VMEM,
        [(2, YY * 8, 128), (X_ROWS, 128), (X_ROWS, 128)],
        [scratch((2, Y_ROWS, 128)), scratch((2, X_ROWS, 128))],
        1_000_000,
    )(grid, y1, y0, ahead)
    x0 = swapped(msg0, "gx", 0)
    x1 = swapped(msg1, "gx", 1)
    weights, rows, depth, across = call(
        ready_kernel,
        [VMEM] * 4,
        VMEM,
        [(CY, 10, 8, 128), (20, 2, MIG), (2, 2, NZ, 2 * MIG, BF16), (2, 2, 8, MIG)],
        [scratch((2, Y_ROWS, 128))],
        10_000_000,
    )(res, cell_count, y1, y0)
    out, face_out, corner_out = call(
        last_kernel,
        [VMEM] * 8,
        HBM,
        [(16, CY, 8, 128), (16, 4, MIG), (16, 4, CORNER)],
        [
            scratch((2, X_ROWS, 128)),
            scratch((2, YY * 8, 128)),
            scratch((3, YP * 8, 128)),
            scratch((3, 3, 3, CY + 2, 8, 128)),
            scratch((16, CY, 8, 128)),
            scratch((16, 4, MIG)),
            scratch((16, 4, CORNER)),
            pltpu.SemaphoreType.DMA((6,)),
        ],
        10_000_000,
    )(res, joined, weights, rows, depth, across, x1, x0)
    out = out.reshape(16, CY, 2, CX, 128).transpose(0, 3, 1, 2, 4).reshape(16, CX, CY * 256)
    return out, face_out, corner_out


def solution(mesh):
    in_specs = (
        P(None, "gx", "gy"),
        P("gx", "gy"),
        P(None, "gx", "gy"),
        P(None, "gx", "gy"),
        P("gx", "gy"),
        P("gx", "gy"),
        P("gx", "gy"),
    )
    out_specs = (P(None, "gx", "gy"), P(None, "gx", "gy"), P(None, "gx", "gy"))
    return jax.shard_map(body, mesh=mesh, in_specs=in_specs, out_specs=out_specs, check_vma=False)
```
